32 devices in a mesh: groups: 2 (over y), shot: 4 (over z), depth: 2 (over x), freq: 2 (over core).
Axes of the slice: x: 2, y: 2, z: 4, core: 2. Of those that a mesh axis runs over, the one named last changes fastest.
Arguments:
- source: float32 [8, 6, 2, 256, 256], P(('groups', 'shot'), 'freq'), parts along dimension 0, may hold values from -6 to 6
- receiver: float32 [8, 6, 2, 256, 256], P(('groups', 'shot'), 'freq'), parts along dimension 0, may hold values from -6 to 6
- slowness: float32 [8, 4, 256, 256], P(('groups', 'shot'), 'depth'), parts along dimension 0, may hold values from 0.6 to 1.4
- omegas: float32 [8, 6], P(('groups', 'shot'), 'freq'), parts along dimension 0, may hold values from 0.5 to 2.5
- shot_start: int32 [8], P(('groups', 'shot')), parts along dimension 0, may hold values from 0 to 256, as said below
Outputs:
- image: float32 [1024, 4, 256], P(('groups', 'shot'), 'depth', 'freq'), parts along dimension 0
The draws below stay inside these ranges and needn't reach their ends.
There are 2 independent parts, one for each index of `groups`. The reference program is written for one: setup_inputs(seed, part) draws one part's arguments, and reference() takes and returns one part's arrays. A program takes and returns all parts, laid end to end along the dimension named above; each array names one. Nothing has to cross between parts.
Inputs may be any that keep to these rules, and one draw needn't show every extreme that they name: `shot_start`: any shot group's aperture may begin at any column of the survey. Shot group 4 // 2 begins at column 0 and shot group 0 at 256.
All inputs are finite; a program needn't handle non-finite values.
Results may differ from the reference program's by a relative error of at most 0.03.
Values may be sent and summed in bfloat16 or wider, within the bound.
A program may use at most 64 MiB of HBM per device.

```python
import math
import jax
import jax.numpy as jnp
from jax import lax

AP = 256
FRONTS = 6
NSHOTS = 4
NZ = 4
IMG_X = 512


def draw_shot_start(key, part):
    positions = jnp.arange(NSHOTS, dtype=jnp.int32)
    begins = jax.random.randint(jax.random.fold_in(key, 11), (NSHOTS,), 0, IMG_X - AP + 1, dtype=jnp.int32)
    begins = jnp.where(positions == NSHOTS // 2, 0, begins)
    begins = jnp.where(positions == 0, IMG_X - AP, begins)
    return begins.astype(jnp.int32)


def block_scale(stream_key, extent, shards, smallest, high):
    def one(position, shards_of):
        draws = jax.random.uniform(jax.random.fold_in(jax.random.fold_in(stream_key, 6), position), (shards_of,), jnp.float32, smallest / len(shards), high / len(shards))
        return jnp.repeat(jnp.exp(draws), extent[position] // shards_of).reshape((-1,) + (1,) * (len(extent) - position - 1))

    level = one(*shards[0])
    for cut in shards[1:]:
        level = level * one(*cut)
    return level


def normal_values(rng, shape, deviation, reach, cuts=(), held_as=jnp.bfloat16):
    values = jax.random.normal(rng, shape, jnp.float32) * deviation
    if len(cuts) > 0:
        values = block_scale(rng, shape, cuts, -0.22, 0.18) * values
    return jnp.clip(values, min=-reach, max=reach).astype(held_as)


def setup_inputs(seed: int = 0, part: int = 0) -> dict:
    arg_keys = jax.random.split(jax.random.key(seed), 6)
    part_keys = jax.random.split(jax.random.fold_in(arg_keys[5], part), 6)
    source = normal_values(part_keys[0], (NSHOTS, FRONTS, 2, AP, AP), 1.0, 6.0, ((0, 4), (1, 2)), jnp.float32)
    receiver = normal_values(part_keys[1], (NSHOTS, FRONTS, 2, AP, AP), 1.0, 6.0, ((0, 4), (1, 2)), jnp.float32)
    slowness = jnp.clip(jnp.exp(math.log(1.4) - 0.8472978 * jax.random.uniform(part_keys[2], (NSHOTS, NZ, AP, AP), jnp.float32) ** block_scale(part_keys[2], (NSHOTS, NZ, AP, AP), ((0, 4), (1, 2)), -0.2, 0.2)), 0.6, 1.4)
    omegas = jnp.clip(jnp.exp(math.log(2.5) - 1.609438 * jax.random.uniform(part_keys[3], (NSHOTS, FRONTS), jnp.float32) ** block_scale(part_keys[3], (NSHOTS, FRONTS), ((0, 4), (1, 2)), -0.2, 0.2)), 0.5, 2.5)
    shot_start = draw_shot_start(jax.random.fold_in(jax.random.fold_in(arg_keys[5], part), 71), part)
    return dict(source=source, receiver=receiver, slowness=slowness, omegas=omegas, shot_start=shot_start)


def tables(points):
    positions = jnp.arange(points, dtype=jnp.int32)
    product = positions[:, None] * positions[None, :] % points
    angles = 2.0 * jnp.pi / points * product.astype(jnp.float32)
    cosine_table = jnp.cos(angles).astype(jnp.bfloat16)
    sine_table = jnp.sin(angles).astype(jnp.bfloat16)
    forward = jnp.concatenate([jnp.concatenate([cosine_table, -sine_table], axis=1), jnp.concatenate([sine_table, cosine_table], axis=1)], axis=0)
    inverse = jnp.concatenate([jnp.concatenate([cosine_table, sine_table], axis=1), jnp.concatenate([-sine_table, cosine_table], axis=1)], axis=0)
    return (forward, inverse)

def lateral_grids(points):
    positions = jnp.arange(points, dtype=jnp.int32)
    wrapped = (positions + points // 2) % points - points // 2
    wavenumber = 2.0 * jnp.pi / points * wrapped.astype(jnp.float32)
    edge_width = points // 16
    distance_in = jnp.minimum(positions, points - 1 - positions) + 1
    edge_taper = jnp.minimum(distance_in.astype(jnp.float32) / edge_width, 1.0)
    return (wavenumber, edge_taper)

def flip_parts(field_in):
    leading = field_in.shape[:-2]
    row_count = field_in.shape[-2]
    col_count = field_in.shape[-1] // 2
    pieces = field_in.reshape(leading + (row_count, 2, col_count))
    moved = jnp.swapaxes(pieces, -3, -1)
    return moved.reshape(leading + (col_count, 2 * row_count))

def extrapolate(wave_state, slow_level, angular, field_signs, forward, inverse, wavenumber, edge_taper):
    batch_size, points, width = wave_state.shape
    inv_points = 1.0 / points
    half_done = jnp.dot(wave_state.reshape(batch_size * points, width), forward, preferred_element_type=jnp.float32)
    half_done = flip_parts(half_done.astype(jnp.bfloat16).reshape(batch_size, points, width))
    spectrum = jnp.dot(half_done.reshape(batch_size * points, width), forward, preferred_element_type=jnp.float32).reshape(batch_size, points, width)
    mean_slow = jnp.mean(slow_level)
    radius_sq = jnp.square(angular * mean_slow)
    square = jnp.square(wavenumber)[:, None] + jnp.square(wavenumber)[None, :]
    vertical = radius_sq[:, None, None] - square[None]
    real_kz = jnp.sqrt(jnp.maximum(vertical, 0.0))
    damping = jnp.exp(-jnp.sqrt(jnp.maximum(-vertical, 0.0)))
    phase_turn = field_signs[:, None, None] * real_kz
    phase_real = damping * jnp.cos(phase_turn)
    phase_imag = damping * jnp.sin(phase_turn)
    spec_real = spectrum[..., :points]
    spec_imag = spectrum[..., points:]
    shifted = jnp.concatenate([spec_real * phase_real - spec_imag * phase_imag, spec_real * phase_imag + spec_imag * phase_real], axis=-1).astype(jnp.bfloat16)
    half_back = jnp.dot(shifted.reshape(batch_size * points, width), inverse, preferred_element_type=jnp.float32) * inv_points
    half_back = flip_parts(half_back.astype(jnp.bfloat16).reshape(batch_size, points, width))
    field_out = jnp.dot(half_back.reshape(batch_size * points, width), inverse, preferred_element_type=jnp.float32).reshape(batch_size, points, width) * inv_points
    correction = (field_signs * angular)[:, None, None] * (slow_level - mean_slow)[None]
    window = edge_taper[:, None] * edge_taper[None, :]
    corr_real = jnp.cos(correction) * window[None]
    corr_imag = jnp.sin(correction) * window[None]
    field_real = field_out[..., :points]
    field_imag = field_out[..., points:]
    return (field_real * corr_real - field_imag * corr_imag, field_real * corr_imag + field_imag * corr_real)

def reference(source, receiver, slowness, omegas, shot_start):
    points = source.shape[-1]
    fronts = source.shape[1]
    forward, inverse = tables(points)
    wavenumber, edge_taper = lateral_grids(points)
    field_signs = jnp.tile(jnp.array([-1.0, 1.0], jnp.float32), fronts)

    def one_shot(image_sum, shot_data):
        src_shot, rcv_shot, slow_shot, rate_shot, begin = shot_data
        paired = jnp.stack([src_shot, rcv_shot], axis=1)
        joined = jnp.concatenate([paired[:, :, 0], paired[:, :, 1]], axis=-1)
        wave_state = joined.reshape(fronts * 2, points, 2 * points).astype(jnp.bfloat16)
        angular = jnp.repeat(rate_shot, 2)

        def one_level(level_state, slow_level):
            real_part, imag_part = extrapolate(level_state, slow_level, angular, field_signs, forward, inverse, wavenumber, edge_taper)
            real_pair = real_part.reshape(fronts, 2, points, points)
            imag_pair = imag_part.reshape(fronts, 2, points, points)
            level_term = lax.optimization_barrier(jnp.sum(real_pair[:, 0] * real_pair[:, 1] + imag_pair[:, 0] * imag_pair[:, 1], axis=0))
            new_state = jnp.concatenate([real_part, imag_part], axis=-1).astype(jnp.bfloat16)
            return (new_state, level_term)
        final_state, level_terms = lax.scan(one_level, wave_state, slow_shot)
        placed = jnp.transpose(level_terms, (1, 0, 2))
        begin_row = begin.astype(jnp.int32)
        zero_index = jnp.zeros((), jnp.int32)
        current = lax.dynamic_slice(image_sum, (begin_row, zero_index, zero_index), placed.shape)
        image_sum = lax.dynamic_update_slice(image_sum, current + placed, (begin_row, zero_index, zero_index))
        return (image_sum, zero_index)
    initial = jnp.zeros((IMG_X, NZ, points), jnp.float32)
    image_sum, unused_out = lax.scan(one_shot, initial, (source, receiver, slowness, omegas, shot_start))
    return image_sum
```

```python
import functools

import jax
import jax.numpy as jnp
import ml_dtypes
import numpy as np
from jax import lax
from jax.experimental import pallas as pl
from jax.experimental.pallas import tpu as pltpu
from jax.sharding import PartitionSpec as P

TILE = 128


def from_behind(array, axis, by):
    peers = lax.axis_size(axis)
    pairs = [(i, i + by) for i in range(peers) if 0 <= i + by < peers]
    return lax.ppermute(array, axis, pairs)


def tables(points):
    positions = jnp.arange(points, dtype=jnp.int32)
    product = positions[:, None] * positions[None, :] % points
    angles = 2.0 * jnp.pi / points * product.astype(jnp.float32)
    cosine_table = jnp.cos(angles).astype(jnp.bfloat16)
    sine_table = jnp.sin(angles).astype(jnp.bfloat16)
    forward = jnp.concatenate(
        [
            jnp.concatenate([cosine_table, -sine_table], axis=1),
            jnp.concatenate([sine_table, cosine_table], axis=1),
        ],
        axis=0,
    )
    inverse = jnp.concatenate(
        [
            jnp.concatenate([cosine_table, sine_table], axis=1),
            jnp.concatenate([-sine_table, cosine_table], axis=1),
        ],
        axis=0,
    )
    return (forward, inverse)


def lateral_grids(points):
    positions = jnp.arange(points, dtype=jnp.int32)
    wrapped = (positions + points // 2) % points - points // 2
    wavenumber = 2.0 * jnp.pi / points * wrapped.astype(jnp.float32)
    edge_width = points // 16
    distance_in = jnp.minimum(positions, points - 1 - positions) + 1
    edge_taper = jnp.minimum(distance_in.astype(jnp.float32) / edge_width, 1.0)
    return (wavenumber, edge_taper)


def flip_parts(field_in):
    leading = field_in.shape[:-2]
    row_count = field_in.shape[-2]
    col_count = field_in.shape[-1] // 2
    pieces = field_in.reshape(leading + (row_count, 2, col_count))
    moved = jnp.swapaxes(pieces, -3, -1)
    return moved.reshape(leading + (col_count, 2 * row_count))


def extrapolate(
    wave_state, slow_level, angular, field_signs, forward, inverse, wavenumber, edge_taper
):
    batch_size, points, width = wave_state.shape
    inv_points = 1.0 / points
    half_done = jnp.dot(
        wave_state.reshape(batch_size * points, width), forward, preferred_element_type=jnp.float32
    )
    half_done = flip_parts(half_done.astype(jnp.bfloat16).reshape(batch_size, points, width))
    spectrum = jnp.dot(
        half_done.reshape(batch_size * points, width), forward, preferred_element_type=jnp.float32
    ).reshape(batch_size, points, width)
    mean_slow = jnp.mean(slow_level)
    radius_sq = jnp.square(angular * mean_slow)
    square = jnp.square(wavenumber)[:, None] + jnp.square(wavenumber)[None, :]
    vertical = radius_sq[:, None, None] - square[None]
    real_kz = jnp.sqrt(jnp.maximum(vertical, 0.0))
    damping = jnp.exp(-jnp.sqrt(jnp.maximum(-vertical, 0.0)))
    phase_turn = field_signs[:, None, None] * real_kz
    phase_real = damping * jnp.cos(phase_turn)
    phase_imag = damping * jnp.sin(phase_turn)
    spec_real = spectrum[..., :points]
    spec_imag = spectrum[..., points:]
    shifted = jnp.concatenate(
        [
            spec_real * phase_real - spec_imag * phase_imag,
            spec_real * phase_imag + spec_imag * phase_real,
        ],
        axis=-1,
    ).astype(jnp.bfloat16)
    half_back = (
        jnp.dot(
            shifted.reshape(batch_size * points, width), inverse, preferred_element_type=jnp.float32
        )
        * inv_points
    )
    half_back = flip_parts(half_back.astype(jnp.bfloat16).reshape(batch_size, points, width))
    field_out = (
        jnp.dot(
            half_back.reshape(batch_size * points, width),
            inverse,
            preferred_element_type=jnp.float32,
        ).reshape(batch_size, points, width)
        * inv_points
    )
    correction = (field_signs * angular)[:, None, None] * (slow_level - mean_slow)[None]
    window = edge_taper[:, None] * edge_taper[None, :]
    corr_real = jnp.cos(correction) * window[None]
    corr_imag = jnp.sin(correction) * window[None]
    field_real = field_out[..., :points]
    field_imag = field_out[..., points:]
    return (
        field_real * corr_real - field_imag * corr_imag,
        field_real * corr_imag + field_imag * corr_real,
    )


def local(source, receiver, slowness, omegas, shot_start):
    points = source.shape[-1]
    fronts = source.shape[1]
    levels = slowness.shape[1]
    segments = lax.axis_size("depth")
    segment_index = lax.axis_index("depth")
    forward, inverse = tables(points)
    wavenumber, edge_taper = lateral_grids(points)
    field_signs = jnp.array([-1.0, 1.0], jnp.float32)

    def surface(chosen):
        src_front = lax.dynamic_index_in_dim(source[0], chosen, 0, keepdims=False)
        rcv_front = lax.dynamic_index_in_dim(receiver[0], chosen, 0, keepdims=False)
        paired = jnp.stack([src_front, rcv_front])
        return jnp.concatenate([paired[:, 0], paired[:, 1]], axis=-1).astype(jnp.bfloat16)

    def extrapolate_front(operands):
        wave_state, rate_now = operands
        angular = jnp.stack([rate_now, rate_now])
        level_terms = []
        for level_index in range(levels):
            real_part, imag_part = extrapolate(
                wave_state,
                slowness[0, level_index],
                angular,
                field_signs,
                forward,
                inverse,
                wavenumber,
                edge_taper,
            )
            level_terms.append(real_part[0] * real_part[1] + imag_part[0] * imag_part[1])
            wave_state = jnp.concatenate([real_part, imag_part], axis=-1).astype(jnp.bfloat16)
        return (wave_state, jnp.stack(level_terms, axis=1))

    def stay_still(operands):
        wave_state, rate_now = operands
        return (jnp.zeros_like(wave_state), jnp.zeros((points, levels, points), jnp.float32))

    def one_turn(turn_index, carry):
        incoming, image_sum = carry
        front_index = turn_index - segment_index
        active = jnp.logical_and(front_index >= 0, front_index < fronts)
        chosen = jnp.clip(front_index, 0, fronts - 1)
        begin_field = jnp.where(segment_index == 0, surface(chosen), incoming)
        rate_now = lax.dynamic_index_in_dim(omegas[0], chosen, 0, keepdims=False)
        wave_state, level_image = lax.cond(
            active, extrapolate_front, stay_still, (begin_field, rate_now)
        )
        incoming = from_behind(wave_state, "depth", 1)
        return (incoming, image_sum + level_image)

    initial = (
        jnp.zeros((2, points, 2 * points), jnp.bfloat16),
        jnp.zeros((points, levels, points), jnp.float32),
    )
    final_carry = lax.fori_loop(0, segments + fronts - 1, one_turn, initial)
    local_image = lax.psum_scatter(
        final_carry[1].astype(jnp.bfloat16), "freq", scatter_dimension=2, tiled=True
    ).astype(jnp.float32)
    aperture_start = shot_start[0]
    owners = lax.axis_size("shot")
    survey_cols = owners * TILE
    padding = jnp.zeros((survey_cols,) + local_image.shape[1:], jnp.float32)
    padded = jnp.concatenate([padding, local_image, padding], axis=0)
    offset = jnp.clip(
        jnp.zeros((), jnp.int32) - aperture_start + survey_cols, 0, points + survey_cols
    )
    placed = lax.dynamic_slice_in_dim(padded, offset, survey_cols, 0)
    blocks = placed.reshape((owners, TILE) + local_image.shape[1:])
    received = lax.all_to_all(
        blocks.astype(jnp.bfloat16), "shot", split_axis=0, concat_axis=0, tiled=True
    ).astype(blocks.dtype)
    collected = jnp.sum(received, axis=0)
    return collected


MESH = pl.DeviceIdType.MESH
BF16 = jnp.bfloat16
F32 = jnp.float32
SLOWEST, SLOWNESS_SPAN, FASTEST_TURN = 1.4, 0.8, 2.5


def even_polynomial(function, limit, degree):
    series = np.polynomial.chebyshev.Chebyshev.interpolate(
        lambda x: function(np.sqrt(np.maximum(x, 0.0))), degree, domain=[0.0, limit]
    )
    return [float(c) for c in series.convert(kind=np.polynomial.Polynomial).coef]


def horner(coefficients, x):
    total = coefficients[-1] * x + coefficients[-2]
    for c in coefficients[-3::-1]:
        total = total * x + c
    return total


def sinc(y):
    return np.sinc(y / np.pi)


def fold_order(points):
    half = points // 2
    even = list(range(0, half, 2)) + [half] + list(range(points - 2, half, -2))
    odd = list(range(1, half, 2)) + list(range(points - 1, half, -2))
    return np.array(even), np.array(odd)


def fold_tables(points):
    half = points // 2
    positions = np.arange(points)
    angles = 2.0 * np.pi / points * (positions[:, None] * positions[None, :] % points)
    cosine, sine = np.cos(angles), np.sin(angles)
    right_forward, left_forward, left_inverse, right_inverse = [], [], [], []
    for order in fold_order(points):
        c, s = cosine[:half, order], sine[:half, order]
        right_forward.append(np.block([[c, -s], [s, c]]))
        left_forward.append(np.block([[c.T, s.T], [-s.T, c.T]]))
        left_inverse.append(np.block([[c, -s], [s, c]]))
        right_inverse.append(np.block([[c.T, s.T], [-s.T, c.T]]))
    return [
        np.stack(t).astype(ml_dtypes.bfloat16)
        for t in (right_forward, left_forward, left_inverse, right_inverse)
    ]


def fold_grids(points):
    wrapped = (np.arange(points) + points // 2) % points - points // 2
    squared = np.square(2.0 * np.pi / points * wrapped)[np.concatenate(fold_order(points))]
    square = (squared[:, None] + squared[None, :]).astype(np.float32)
    distance_in = np.minimum(np.arange(points), points - 1 - np.arange(points)) + 1
    taper = np.minimum(distance_in / (points // 16), 1.0)
    window = (taper[:, None] * taper[None, :] / points).astype(np.float32)
    return square, window


def migrate_kernel(
    dims, source, receiver, slowness, omegas, start, rf, lf, li, ri, square, window, image,
    fbuf, st, stx, ds, s0, om, pr, pi, cr, ci, bb, ww, xx, uq, acc, accb, shq, accr, shr, chip,
    xsend, xrecv, zsend, zrecv,
    load_sem, ds_sem, s0_sem, sh_sem, om_sem, acc_sem, shq_sem, x_sem, zs_sem, zr_sem,
):
    points, levels, shots, fronts = dims
    half, quarter = points // 2, points // 4
    total_levels = 2 * levels
    d, f, s = lax.axis_index("depth"), lax.axis_index("freq"), lax.axis_index("shot")
    other_core, other_chip = {"freq": 1 - f}, {"depth": 1 - d}
    provider = f == d

    barrier = pltpu.get_barrier_semaphore()
    pl.semaphore_signal(barrier, inc=1, device_id=other_core, device_id_type=MESH)
    pl.semaphore_signal(barrier, inc=1, device_id=other_chip, device_id_type=MESH)
    for step in range(1, shots):
        pl.semaphore_signal(
            barrier, inc=1, device_id={"shot": lax.rem(s + step, shots)}, device_id_type=MESH
        )

    def load(index, front, field):
        return pltpu.make_async_copy(field.at[0, front], fbuf.at[index], load_sem.at[index])

    def remote(source_ref, target_ref, sems, device, index):
        return pltpu.make_async_remote_copy(
            src_ref=source_ref, dst_ref=target_ref, send_sem=sems.at[0, index],
            recv_sem=sems.at[1, index], device_id=device, device_id_type=MESH,
        )

    def send_field():
        return remote(stx, st.at[2], sh_sem, other_core, 0)

    def send_turn():
        return remote(om, om, om_sem, other_core, 0)

    def send_slow(z):
        return remote(ds.at[z], ds.at[z], ds_sem, other_chip, z)

    def send_mean(z):
        return remote(s0.at[z], s0.at[z], s0_sem, other_chip, z)

    def send_image(z):
        return remote(accb.at[z, 1 - f], accr.at[z], acc_sem, other_core, z)

    def send_shared(z):
        return remote(shq.at[z, 1 - f], shr.at[z], shq_sem, other_core, z)

    def send_section(z):
        j = lax.rem(z, levels)
        return remote(xsend.at[j], xrecv.at[j], x_sem, other_chip, j)

    def send_columns(j, step):
        owner = lax.rem(s + step, shots)
        return pltpu.make_async_remote_copy(
            src_ref=zsend.at[j, owner], dst_ref=zrecv.at[j, s], send_sem=zs_sem.at[j, owner],
            recv_sem=zr_sem.at[j, s], device_id={"shot": owner}, device_id_type=MESH,
        )

    def recv_columns(j, step):
        owner = lax.rem(s + step, shots)
        return pltpu.make_async_remote_copy(
            src_ref=zsend.at[j, owner], dst_ref=zrecv.at[j, owner], send_sem=zs_sem.at[j, owner],
            recv_sem=zr_sem.at[j, owner], device_id={"shot": owner}, device_id_type=MESH,
        )

    load(0, d, source).start()
    load(1, d, receiver).start()

    @pl.when(provider)
    def _():
        load(2, fronts - 1, source).start()
        load(3, fronts - 1, receiver).start()

    for j in range(levels):
        mean = jnp.mean(slowness[0, j])
        ds[d * levels + j] = (slowness[0, j] - mean).astype(BF16)
        s0[d * levels + j] = jnp.full((8, points), mean, F32)

    pl.semaphore_wait(barrier, shots + 1)
    for j in range(levels):
        send_mean(d * levels + j).start()
        send_slow(d * levels + j).start()

    def fold_into(target, re, im):
        lo, hi = slice(0, half), slice(half, points)
        target[0, :, lo] = (re[:, lo] + re[:, hi]).astype(BF16)
        target[0, :, hi] = (im[:, lo] + im[:, hi]).astype(BF16)
        target[1, :, lo] = (re[:, lo] - re[:, hi]).astype(BF16)
        target[1, :, hi] = (im[:, lo] - im[:, hi]).astype(BF16)

    @pl.when(provider)
    def _():
        om[...] = jnp.full((8, points), omegas[0, fronts - 1], F32)
        send_turn().start()
        load(2, fronts - 1, source).wait()
        load(3, fronts - 1, receiver).wait()
        fold_into(stx, fbuf[3 - f, 0], fbuf[3 - f, 1])
        send_field().start()
        fold_into(st.at[2], fbuf[2 + f, 0], fbuf[2 + f, 1])

    for index, field in enumerate((source, receiver)):
        load(index, d, field).wait()
        fold_into(st.at[index], fbuf[index, 0], fbuf[index, 1])

    @pl.when(jnp.logical_not(provider))
    def _():
        send_turn().wait_recv()
        send_field().wait_recv()

    turn_own = omegas[0, d]
    sign = (2 * f - 1).astype(F32)
    limit = 1.01 * (FASTEST_TURN * SLOWEST) ** 2
    kz_cos = even_polynomial(np.cos, limit, 6)
    kz_sinc = even_polynomial(sinc, limit, 6)
    limit = 1.01 * (FASTEST_TURN * SLOWNESS_SPAN) ** 2
    turn_cos = even_polynomial(np.cos, limit, 4)
    turn_sinc = even_polynomial(sinc, limit, 4)
    inv = 1.0 / points

    def propagator(index, radius_sq, flip):
        def rows(at, count, targets):
            vertical = radius_sq - square[at : at + count, :]
            root = jnp.sqrt(jnp.abs(vertical))
            positive = vertical >= 0.0
            x = jnp.maximum(vertical, 0.0)
            re = jnp.where(positive, horner(kz_cos, x), jnp.exp(-root)) * inv
            im = jnp.where(positive, root * horner(kz_sinc, x), 0.0) * (inv * flip)
            for target in targets:
                pr[index, target : target + count, :] = re
                pi[index, target : target + count, :] = im

        step = quarter // 2
        for at in range(0, quarter, step):
            rows(at, step, (at, at + quarter))
            rows(half + at, step, (half + at, half + quarter + at))
        rows(quarter, 8, (quarter,))

    def correction(index, turn, slow):
        step = quarter // 2
        for at in range(0, points, step):
            x = turn * slow[at : at + step, :].astype(F32)
            y = x * x
            w = window[at : at + step, :]
            cr[index, at : at + step, :] = horner(turn_cos, y) * w
            ci[index, at : at + step, :] = horner(turn_sinc, y) * (x * w)

    def dot(a, b):
        return jnp.dot(a, b, preferred_element_type=F32)

    def transform(i):
        for part in range(2):
            v = dot(st[i, part], rf[part])
            top, bottom = v[:half], v[half:]
            lanes = slice(part * half, (part + 1) * half)
            for fold, w in ((0, top + bottom), (1, top - bottom)):
                bb[i, fold, :half, lanes] = w[:, :half].astype(BF16)
                bb[i, fold, half:, lanes] = w[:, half:].astype(BF16)

    def advance(i, which, sigma):
        for part in range(2):
            w = dot(lf[part], bb[i, part])
            rows = slice(part * half, (part + 1) * half)
            re, im = w[:half], w[half:]
            p, q = pr[which, rows, :], pi[which, rows, :]
            if sigma > 0:
                ww[i, part, :half, :] = (re * p - im * q).astype(BF16)
                ww[i, part, half:, :] = (re * q + im * p).astype(BF16)
            else:
                ww[i, part, :half, :] = (re * p + im * q).astype(BF16)
                ww[i, part, half:, :] = (im * p - re * q).astype(BF16)

    def back(i):
        even, odd = dot(li[0], ww[i, 0]), dot(li[1], ww[i, 1])
        for rows, y in ((slice(0, half), even + odd), (slice(half, points), even - odd)):
            for part in range(2):
                lanes = slice(part * half, (part + 1) * half)
                xx[i, part, rows, :half] = y[:half, lanes].astype(BF16)
                xx[i, part, rows, half:] = y[half:, lanes].astype(BF16)

    def finish(i, which, sigma):
        even, odd = dot(xx[i, 0], ri[0]), dot(xx[i, 1], ri[1])
        out = []
        for lanes, y in ((slice(0, half), even + odd), (slice(half, points), even - odd)):
            re, im = y[:, :half], y[:, half:]
            c, t = cr[which, :, lanes], ci[which, :, lanes]
            if sigma > 0:
                out.append((re * c - im * t, re * t + im * c))
            else:
                out.append((re * c + im * t, im * c - re * t))
        for fold in range(2):
            for which_part in range(2):
                a, b = out[0][which_part], out[1][which_part]
                lanes = slice(which_part * half, (which_part + 1) * half)
                st[i, fold, :, lanes] = (a + b if fold == 0 else a - b).astype(BF16)
        return out

    def combine(z):
        send_image(z).wait_recv()
        send_shared(z).wait_recv()
        total = acc[lax.rem(z, 2), f] + accr[z].astype(F32)
        total += shq[z, f, 0].astype(F32) * shr[z, 0].astype(F32)
        total += shq[z, f, 1].astype(F32) * shr[z, 1].astype(F32)
        mine = lax.div(z, levels) == d

        @pl.when(mine)
        def _():
            chip[lax.rem(z, levels)] = total

        @pl.when(jnp.logical_not(mine))
        def _():
            xsend[lax.rem(z, levels)] = total.astype(BF16)
            send_section(z).start()

    def place(z):
        j = lax.rem(z, levels)
        send_section(z).wait_recv()
        total = (chip[j] + xrecv[j].astype(F32)).astype(BF16)
        columns = lax.broadcasted_iota(jnp.int32, (TILE, points), 0)
        places = lax.broadcasted_iota(jnp.int32, (TILE, points), 1)
        for owner in range(shots):
            chosen = places == columns + (owner * TILE - start[0])
            chosen = jnp.where(chosen, 1.0, 0.0).astype(BF16)
            zsend[j, owner] = dot(chosen, total).astype(BF16)
        for step in range(1, shots):
            send_columns(j, step).start()

    def one_level(z, carry):
        mine = lax.div(z, levels) == d

        @pl.when(jnp.logical_not(mine))
        def _():
            send_mean(z).wait_recv()
            send_slow(z).wait_recv()

        mean = s0[z][0:1, :]
        turn_shared = om[0:1, :]
        transform(2)
        propagator(1, jnp.square(turn_shared * mean), sign)
        correction(1, sign * turn_shared, ds[z])
        transform(0)
        transform(1)
        propagator(0, jnp.square(turn_own * mean), 1.0)
        correction(0, turn_own, ds[z])
        advance(2, 1, 1)
        back(2)
        advance(0, 0, -1)
        advance(1, 0, 1)

        @pl.when(z >= 1)
        def _():
            combine(z - 1)

        shared = finish(2, 1, 1)
        for side in range(2):
            for part in range(2):
                shq[z, side, part] = shared[side][part].astype(BF16)
        send_shared(z).start()
        back(0)
        back(1)
        first = finish(0, 0, -1)
        for side in range(2):
            for part in range(2):
                uq[side, part] = first[side][part]
        second = finish(1, 0, 1)
        for side in range(2):
            product = uq[side, 0] * second[side][0] + uq[side, 1] * second[side][1]
            acc[lax.rem(z, 2), side] = product
            accb[z, side] = product.astype(BF16)
        send_image(z).start()

        @pl.when(jnp.logical_and(z >= 1, lax.div(z - 1, levels) == d))
        def _():
            place(z - 1)

        return carry

    lax.fori_loop(0, total_levels, one_level, 0)
    last = total_levels - 1
    combine(last)

    @pl.when(lax.div(last, levels) == d)
    def _():
        place(last)

    for j in range(levels):
        total = zsend[j, s].astype(F32)
        for step in range(1, shots):
            recv_columns(j, step).wait_recv()
            total += zrecv[j, lax.rem(s + step, shots)].astype(F32)
        image[:, j, :] = total

    @pl.when(provider)
    def _():
        send_turn().wait_send()
        send_field().wait_send()

    for j in range(levels):
        send_mean(d * levels + j).wait_send()
        send_slow(d * levels + j).wait_send()
        send_section((1 - d) * levels + j).wait_send()
        for step in range(1, shots):
            send_columns(j, step).wait_send()
    for z in range(total_levels):
        send_image(z).wait_send()
        send_shared(z).wait_send()


def migrate(source, receiver, slowness, omegas, shot_start):
    points = source.shape[-1]
    fronts = source.shape[1]
    levels = slowness.shape[1]
    shots = lax.axis_size("shot")
    total = 2 * levels
    half = points // 2
    tables_in = [jnp.asarray(t) for t in fold_tables(points)]
    grids_in = [jnp.asarray(t) for t in fold_grids(points)]
    full = (points, points)
    side = (points, half)
    vmem, sem = pltpu.VMEM, pltpu.SemaphoreType.DMA
    in_vmem = pl.BlockSpec(memory_space=pltpu.VMEM)
    in_smem = pl.BlockSpec(memory_space=pltpu.SMEM)
    anywhere = pl.BlockSpec(memory_space=pl.ANY)
    return pl.pallas_call(
        functools.partial(migrate_kernel, (points, levels, shots, fronts)),
        out_shape=jax.ShapeDtypeStruct((TILE, levels, half), F32),
        in_specs=[anywhere, anywhere, in_vmem, in_smem, in_smem] + [in_vmem] * 6,
        out_specs=in_vmem,
        scratch_shapes=[
            vmem((4, 2) + full, F32),
            vmem((3, 2) + full, BF16),
            vmem((2,) + full, BF16),
            vmem((total,) + full, BF16),
            vmem((total, 8, points), F32),
            vmem((8, points), F32),
            vmem((2,) + full, F32),
            vmem((2,) + full, F32),
            vmem((2,) + full, F32),
            vmem((2,) + full, F32),
            vmem((3, 2) + full, BF16),
            vmem((3, 2) + full, BF16),
            vmem((3, 2) + full, BF16),
            vmem((2, 2) + side, F32),
            vmem((2, 2) + side, F32),
            vmem((total, 2) + side, BF16),
            vmem((total, 2, 2) + side, BF16),
            vmem((total,) + side, BF16),
            vmem((total, 2) + side, BF16),
            vmem((levels,) + side, F32),
            vmem((levels,) + side, BF16),
            vmem((levels,) + side, BF16),
            vmem((levels, shots, TILE, half), BF16),
            vmem((levels, shots, TILE, half), BF16),
            sem((4,)),
            sem((2, total)),
            sem((2, total)),
            sem((2, 1)),
            sem((2, 1)),
            sem((2, total)),
            sem((2, total)),
            sem((2, levels)),
            sem((levels, shots)),
            sem((levels, shots)),
        ],
        compiler_params=pltpu.CompilerParams(
            collective_id=0, has_side_effects=True, vmem_limit_bytes=48 * 1024 * 1024
        ),
        name="migrate",
    )(source, receiver, slowness, omegas, shot_start, *tables_in, *grids_in)


def solution(mesh):
    sizes = mesh.shape

    def per_device(source, *rest):
        if sizes["depth"] == 2 and sizes["freq"] == 2 and source.shape[1] == 3:
            return migrate(source, *rest)
        return local(source, *rest)

    return jax.shard_map(
        per_device,
        mesh=mesh,
        in_specs=(
            P(("groups", "shot"), "freq", None, None, None),
            P(("groups", "shot"), "freq", None, None, None),
            P(("groups", "shot"), "depth", None, None),
            P(("groups", "shot"), "freq"),
            P(("groups", "shot")),
        ),
        out_specs=P(("groups", "shot"), "depth", "freq"),
        check_vma=False,
    )
```

```python
import functools

import jax
import jax.numpy as jnp
import numpy as np
from jax import lax
from jax.experimental import pallas as pl
from jax.experimental.pallas import tpu as pltpu
from jax.sharding import PartitionSpec as P

TILE = 128


def from_behind(array, axis, by):
    peers = lax.axis_size(axis)
    pairs = [(i, i + by) for i in range(peers) if 0 <= i + by < peers]
    return lax.ppermute(array, axis, pairs)


def tables(points):
    positions = jnp.arange(points, dtype=jnp.int32)
    product = positions[:, None] * positions[None, :] % points
    angles = 2.0 * jnp.pi / points * product.astype(jnp.float32)
    cosine_table = jnp.cos(angles).astype(jnp.bfloat16)
    sine_table = jnp.sin(angles).astype(jnp.bfloat16)
    forward = jnp.concatenate(
        [
            jnp.concatenate([cosine_table, -sine_table], axis=1),
            jnp.concatenate([sine_table, cosine_table], axis=1),
        ],
        axis=0,
    )
    inverse = jnp.concatenate(
        [
            jnp.concatenate([cosine_table, sine_table], axis=1),
            jnp.concatenate([-sine_table, cosine_table], axis=1),
        ],
        axis=0,
    )
    return (forward, inverse)


def lateral_grids(points):
    positions = jnp.arange(points, dtype=jnp.int32)
    wrapped = (positions + points // 2) % points - points // 2
    wavenumber = 2.0 * jnp.pi / points * wrapped.astype(jnp.float32)
    edge_width = points // 16
    distance_in = jnp.minimum(positions, points - 1 - positions) + 1
    edge_taper = jnp.minimum(distance_in.astype(jnp.float32) / edge_width, 1.0)
    return (wavenumber, edge_taper)


def flip_parts(field_in):
    leading = field_in.shape[:-2]
    row_count = field_in.shape[-2]
    col_count = field_in.shape[-1] // 2
    pieces = field_in.reshape(leading + (row_count, 2, col_count))
    moved = jnp.swapaxes(pieces, -3, -1)
    return moved.reshape(leading + (col_count, 2 * row_count))


def extrapolate(
    wave_state, slow_level, angular, field_signs, forward, inverse, wavenumber, edge_taper
):
    batch_size, points, width = wave_state.shape
    inv_points = 1.0 / points
    half_done = jnp.dot(
        wave_state.reshape(batch_size * points, width), forward, preferred_element_type=jnp.float32
    )
    half_done = flip_parts(half_done.astype(jnp.bfloat16).reshape(batch_size, points, width))
    spectrum = jnp.dot(
        half_done.reshape(batch_size * points, width), forward, preferred_element_type=jnp.float32
    ).reshape(batch_size, points, width)
    mean_slow = jnp.mean(slow_level)
    radius_sq = jnp.square(angular * mean_slow)
    square = jnp.square(wavenumber)[:, None] + jnp.square(wavenumber)[None, :]
    vertical = radius_sq[:, None, None] - square[None]
    real_kz = jnp.sqrt(jnp.maximum(vertical, 0.0))
    damping = jnp.exp(-jnp.sqrt(jnp.maximum(-vertical, 0.0)))
    phase_turn = field_signs[:, None, None] * real_kz
    phase_real = damping * jnp.cos(phase_turn)
    phase_imag = damping * jnp.sin(phase_turn)
    spec_real = spectrum[..., :points]
    spec_imag = spectrum[..., points:]
    shifted = jnp.concatenate(
        [
            spec_real * phase_real - spec_imag * phase_imag,
            spec_real * phase_imag + spec_imag * phase_real,
        ],
        axis=-1,
    ).astype(jnp.bfloat16)
    half_back = (
        jnp.dot(
            shifted.reshape(batch_size * points, width), inverse, preferred_element_type=jnp.float32
        )
        * inv_points
    )
    half_back = flip_parts(half_back.astype(jnp.bfloat16).reshape(batch_size, points, width))
    field_out = (
        jnp.dot(
            half_back.reshape(batch_size * points, width),
            inverse,
            preferred_element_type=jnp.float32,
        ).reshape(batch_size, points, width)
        * inv_points
    )
    correction = (field_signs * angular)[:, None, None] * (slow_level - mean_slow)[None]
    window = edge_taper[:, None] * edge_taper[None, :]
    corr_real = jnp.cos(correction) * window[None]
    corr_imag = jnp.sin(correction) * window[None]
    field_real = field_out[..., :points]
    field_imag = field_out[..., points:]
    return (
        field_real * corr_real - field_imag * corr_imag,
        field_real * corr_imag + field_imag * corr_real,
    )


def local(source, receiver, slowness, omegas, shot_start):
    points = source.shape[-1]
    fronts = source.shape[1]
    levels = slowness.shape[1]
    segments = lax.axis_size("depth")
    segment_index = lax.axis_index("depth")
    forward, inverse = tables(points)
    wavenumber, edge_taper = lateral_grids(points)
    field_signs = jnp.array([-1.0, 1.0], jnp.float32)

    def surface(chosen):
        src_front = lax.dynamic_index_in_dim(source[0], chosen, 0, keepdims=False)
        rcv_front = lax.dynamic_index_in_dim(receiver[0], chosen, 0, keepdims=False)
        paired = jnp.stack([src_front, rcv_front])
        return jnp.concatenate([paired[:, 0], paired[:, 1]], axis=-1).astype(jnp.bfloat16)

    def extrapolate_front(operands):
        wave_state, rate_now = operands
        angular = jnp.stack([rate_now, rate_now])
        level_terms = []
        for level_index in range(levels):
            real_part, imag_part = extrapolate(
                wave_state,
                slowness[0, level_index],
                angular,
                field_signs,
                forward,
                inverse,
                wavenumber,
                edge_taper,
            )
            level_terms.append(real_part[0] * real_part[1] + imag_part[0] * imag_part[1])
            wave_state = jnp.concatenate([real_part, imag_part], axis=-1).astype(jnp.bfloat16)
        return (wave_state, jnp.stack(level_terms, axis=1))

    def stay_still(operands):
        wave_state, rate_now = operands
        return (jnp.zeros_like(wave_state), jnp.zeros((points, levels, points), jnp.float32))

    def one_turn(turn_index, carry):
        incoming, image_sum = carry
        front_index = turn_index - segment_index
        active = jnp.logical_and(front_index >= 0, front_index < fronts)
        chosen = jnp.clip(front_index, 0, fronts - 1)
        begin_field = jnp.where(segment_index == 0, surface(chosen), incoming)
        rate_now = lax.dynamic_index_in_dim(omegas[0], chosen, 0, keepdims=False)
        wave_state, level_image = lax.cond(
            active, extrapolate_front, stay_still, (begin_field, rate_now)
        )
        incoming = from_behind(wave_state, "depth", 1)
        return (incoming, image_sum + level_image)

    initial = (
        jnp.zeros((2, points, 2 * points), jnp.bfloat16),
        jnp.zeros((points, levels, points), jnp.float32),
    )
    final_carry = lax.fori_loop(0, segments + fronts - 1, one_turn, initial)
    local_image = lax.psum_scatter(
        final_carry[1].astype(jnp.bfloat16), "freq", scatter_dimension=2, tiled=True
    ).astype(jnp.float32)
    aperture_start = shot_start[0]
    owners = lax.axis_size("shot")
    survey_cols = owners * TILE
    padding = jnp.zeros((survey_cols,) + local_image.shape[1:], jnp.float32)
    padded = jnp.concatenate([padding, local_image, padding], axis=0)
    offset = jnp.clip(
        jnp.zeros((), jnp.int32) - aperture_start + survey_cols, 0, points + survey_cols
    )
    placed = lax.dynamic_slice_in_dim(padded, offset, survey_cols, 0)
    blocks = placed.reshape((owners, TILE) + local_image.shape[1:])
    received = lax.all_to_all(
        blocks.astype(jnp.bfloat16), "shot", split_axis=0, concat_axis=0, tiled=True
    ).astype(blocks.dtype)
    collected = jnp.sum(received, axis=0)
    return collected


MESH = pl.DeviceIdType.MESH
BF16 = jnp.bfloat16
CHUNK = 32
F32 = jnp.float32
SLOWEST, SLOWNESS_SPAN, FASTEST_TURN = 1.4, 0.8, 2.5


def even_polynomial(function, limit, degree):
    series = np.polynomial.chebyshev.Chebyshev.interpolate(
        lambda x: function(np.sqrt(np.maximum(x, 0.0))), degree, domain=[0.0, limit]
    )
    return [float(c) for c in series.convert(kind=np.polynomial.Polynomial).coef]


def horner(coefficients, x):
    total = coefficients[-1] * x + coefficients[-2]
    for c in coefficients[-3::-1]:
        total = total * x + c
    return total


def sinc(y):
    return np.sinc(y / np.pi)


def migrate_kernel(
    dims, source, receiver, slowness, omegas, start, image,
    tab, slow, square, window, res, fbuf, st, ds, s0, om, pr, pi, cr, ci, bb, ww, xx, uq, acc, accb, shq, accr, shr, chip,
    xsend, xrecv, zsend, zrecv,
    load_sem, slow_sem, ds_sem, s0_sem, sh_sem, om_sem, acc_sem, shq_sem, x_sem, zs_sem, zr_sem,
):
    points, levels, shots, fronts = dims
    half, quarter = points // 2, points // 4
    total_levels = 2 * levels
    d, f, s = lax.axis_index("depth"), lax.axis_index("freq"), lax.axis_index("shot")
    other_core, other_chip = {"freq": 1 - f}, {"depth": 1 - d}
    provider = f == d

    barrier = pltpu.get_barrier_semaphore()
    pl.semaphore_signal(barrier, inc=1, device_id=other_core, device_id_type=MESH)
    pl.semaphore_signal(barrier, inc=1, device_id=other_chip, device_id_type=MESH)
    for step in range(1, shots):
        pl.semaphore_signal(
            barrier, inc=1, device_id={"shot": lax.rem(s + step, shots)}, device_id_type=MESH
        )

    def load(index, front, field):
        return pltpu.make_async_copy(field.at[0, front], fbuf.at[index], load_sem.at[index])

    def remote(source_ref, target_ref, sems, device, index):
        return pltpu.make_async_remote_copy(
            src_ref=source_ref, dst_ref=target_ref, send_sem=sems.at[0, index],
            recv_sem=sems.at[1, index], device_id=device, device_id_type=MESH,
        )

    def send_field():
        return send_front(source)

    def send_front(field):
        return remote(field.at[0, fronts - 1], fbuf.at[2], sh_sem, other_core, 0)

    def load_slow(j):
        return pltpu.make_async_copy(slowness.at[0, j], slow.at[j], slow_sem.at[j])

    def send_turn():
        return remote(om, om, om_sem, other_core, 0)

    def send_slow(z):
        return remote(ds.at[z], ds.at[z], ds_sem, other_chip, z)

    def send_mean(z):
        return remote(s0.at[z], s0.at[z], s0_sem, other_chip, z)

    def send_image(z):
        return remote(accb.at[z, 1 - f], accr.at[z], acc_sem, other_core, z)

    def send_shared(z):
        return remote(shq.at[z, 1 - f], shr.at[z], shq_sem, other_core, z)

    def send_section(z):
        j = lax.rem(z, levels)
        return remote(xsend.at[j], xrecv.at[j], x_sem, other_chip, j)

    def send_columns(j, step):
        owner = lax.rem(s + step, shots)
        return pltpu.make_async_remote_copy(
            src_ref=zsend.at[j, owner], dst_ref=zrecv.at[j, s], send_sem=zs_sem.at[j, owner],
            recv_sem=zr_sem.at[j, s], device_id={"shot": owner}, device_id_type=MESH,
        )

    def recv_columns(j, step):
        owner = lax.rem(s + step, shots)
        return pltpu.make_async_remote_copy(
            src_ref=zsend.at[j, owner], dst_ref=zrecv.at[j, owner], send_sem=zs_sem.at[j, owner],
            recv_sem=zr_sem.at[j, owner], device_id={"shot": owner}, device_id_type=MESH,
        )

    for j in range(levels):
        load_slow(j).start()
    for front in range(2):
        @pl.when(jnp.logical_and(provider, f == front))
        def _(field=(source, receiver)[front]):
            load(2, fronts - 1, field).start()

    load(0, d, source).start()
    load(1, d, receiver).start()

    def grid_index(axis):
        at = lax.broadcasted_iota(jnp.int32, (points, points), axis)
        odd = jnp.where(at >= half, 1, 0)
        wave = 2 * jnp.where(at - half * odd >= quarter, at - half * odd - quarter, at - half * odd)
        return at, jnp.where(at == quarter, half, wave + odd).astype(F32) * (2.0 * np.pi / points)

    row, row_wave = grid_index(0)
    column, column_wave = grid_index(1)
    square[...] = jnp.square(row_wave) + jnp.square(column_wave)

    table_cos = even_polynomial(np.cos, np.pi**2, 8)
    table_sinc = even_polynomial(sinc, np.pi**2, 8)

    def frequency(axis, part):
        at = lax.broadcasted_iota(jnp.int32, (half, half), axis)
        if part == 1:
            return jnp.where(at < quarter, 2 * at + 1, points - 1 - 2 * (at - quarter))
        mirrored = jnp.where(at == quarter, half, points - 2 * (at - quarter))
        return jnp.where(at < quarter, 2 * at, mirrored)

    for part in range(2):
        for turned in range(2):
            place = lax.broadcasted_iota(jnp.int32, (half, half), turned)
            product = place * frequency(1 - turned, part)
            wrapped = ((product + half) & (points - 1)) - half
            x = wrapped.astype(F32) * (2.0 * np.pi / points)
            cosine = horner(table_cos, x * x).astype(BF16)
            sine = x * horner(table_sinc, x * x)
            upper, lower = ((-sine).astype(BF16), sine.astype(BF16))
            if turned:
                upper, lower = lower, upper
            tab[turned, part, :half, :half] = cosine
            tab[turned, part, half:, half:] = cosine
            tab[turned, part, :half, half:] = upper
            tab[turned, part, half:, :half] = lower

    def taper(at):
        distance_in = (jnp.minimum(at, points - 1 - at) + 1).astype(F32)
        return jnp.minimum(distance_in * (16.0 / points), 1.0)

    window[...] = taper(row) * taper(column) * (1.0 / points)

    pl.semaphore_wait(barrier, shots + 1)
    for front in range(2):
        @pl.when(jnp.logical_and(provider, f == front))
        def _(field=(receiver, source)[front]):
            om[...] = jnp.full((8, points), omegas[0, fronts - 1], F32)
            send_turn().start()
            send_front(field).start()

    for j in range(levels):
        load_slow(j).wait()
        mean = jnp.mean(slow[j])
        ds[d * levels + j] = (slow[j] - mean).astype(BF16)
        s0[d * levels + j] = jnp.full((8, points), mean, F32)
        send_mean(d * levels + j).start()
        send_slow(d * levels + j).start()

    def fold_into(target, re, im):
        lo, hi = slice(0, half), slice(half, points)
        for at in range(0, points, CHUNK):
            rows = slice(at, at + CHUNK)
            for lanes, x in ((lo, re), (hi, im)):
                a, b = x[rows, lo], x[rows, hi]
                target[0, rows, lanes] = (a + b).astype(BF16)
                target[1, rows, lanes] = (a - b).astype(BF16)

    for index, field in enumerate((source, receiver)):
        load(index, d, field).wait()
        fold_into(st.at[index], fbuf.at[index, 0], fbuf.at[index, 1])

    @pl.when(provider)
    def _():
        load(2, fronts - 1, source).wait()

    @pl.when(jnp.logical_not(provider))
    def _():
        send_turn().wait_recv()
        send_field().wait_recv()

    fold_into(st.at[2], fbuf.at[2, 0], fbuf.at[2, 1])

    turn_own = omegas[0, d]
    sign = (2 * f - 1).astype(F32)
    limit = 1.01 * (FASTEST_TURN * SLOWEST) ** 2
    kz_cos = even_polynomial(np.cos, limit, 5)
    kz_sinc = even_polynomial(sinc, limit, 5)
    limit = 1.01 * (FASTEST_TURN * SLOWNESS_SPAN) ** 2
    turn_cos = even_polynomial(np.cos, limit, 4)
    turn_sinc = even_polynomial(sinc, limit, 3)
    inv = 1.0 / points

    def propagator(index, radius_sq, flip):
        def rows(at, count, targets):
            vertical = radius_sq - square[at : at + count, :]
            root = jnp.sqrt(jnp.abs(vertical))
            positive = vertical >= 0.0
            x = jnp.maximum(vertical, 0.0)
            re = jnp.where(positive, horner(kz_cos, x), jnp.exp(-root)) * inv
            im = jnp.where(positive, root * horner(kz_sinc, x), 0.0) * (inv * flip)
            for target in targets:
                pr[index, target : target + count, :] = re
                pi[index, target : target + count, :] = im

        step = quarter // 2
        for at in range(0, quarter, step):
            rows(at, step, (at, at + quarter))
            rows(half + at, step, (half + at, half + quarter + at))
        rows(quarter, 8, (quarter,))

    def correction(index, turn, slow):
        step = quarter // 2
        for at in range(0, points, step):
            x = turn * slow[at : at + step, :].astype(F32)
            y = x * x
            w = window[at : at + step, :]
            cr[index, at : at + step, :] = horner(turn_cos, y) * w
            ci[index, at : at + step, :] = horner(turn_sinc, y) * (x * w)

    def dot(a, b):
        return jnp.dot(a, b, preferred_element_type=F32)

    def transform(i):
        for part in range(2):
            res[i, part] = dot(st[i, part], tab[0, part])
            lanes = slice(part * half, (part + 1) * half)
            for at in range(0, half, CHUNK):
                top = res[i, part, at : at + CHUNK, :]
                bottom = res[i, part, half + at : half + at + CHUNK, :]
                for fold, w in ((0, top + bottom), (1, top - bottom)):
                    bb[i, fold, at : at + CHUNK, lanes] = w[:, :half].astype(BF16)
                    bb[i, fold, half + at : half + at + CHUNK, lanes] = w[:, half:].astype(BF16)

    def advance(i, which, sigma):
        for part in range(2):
            res[i, part] = dot(tab[1, part], bb[i, part])
            for at in range(0, half, CHUNK):
                rows = slice(part * half + at, part * half + at + CHUNK)
                top, bottom = slice(at, at + CHUNK), slice(half + at, half + at + CHUNK)
                re, im = res[i, part, top, :], res[i, part, bottom, :]
                p, q = pr[which, rows, :], pi[which, rows, :]
                if sigma > 0:
                    ww[i, part, top, :] = (re * p - im * q).astype(BF16)
                    ww[i, part, bottom, :] = (re * q + im * p).astype(BF16)
                else:
                    ww[i, part, top, :] = (re * p + im * q).astype(BF16)
                    ww[i, part, bottom, :] = (im * p - re * q).astype(BF16)

    def back(i):
        for part in range(2):
            res[i, part] = dot(tab[0, part], ww[i, part])
        for at in range(0, points, CHUNK):
            rows = slice(at, at + CHUNK)
            even, odd = res[i, 0, rows, :], res[i, 1, rows, :]
            target = at % half
            lanes = slice(0, half) if at < half else slice(half, points)
            for start_row, y in ((0, even + odd), (half, even - odd)):
                into = slice(start_row + target, start_row + target + CHUNK)
                xx[i, 0, into, lanes] = y[:, :half].astype(BF16)
                xx[i, 1, into, lanes] = y[:, half:].astype(BF16)

    def finish(i, which, sigma, emit):
        for part in range(2):
            res[i, part] = dot(xx[i, part], tab[1, part])
        for at in range(0, points, CHUNK):
            rows = slice(at, at + CHUNK)
            even, odd = res[i, 0, rows, :], res[i, 1, rows, :]
            out = []
            for lanes, y in ((slice(0, half), even + odd), (slice(half, points), even - odd)):
                re, im = y[:, :half], y[:, half:]
                c, t = cr[which, rows, lanes], ci[which, rows, lanes]
                if sigma > 0:
                    out.append((re * c - im * t, re * t + im * c))
                else:
                    out.append((re * c + im * t, im * c - re * t))
            for part in range(2):
                a, b = out[0][part], out[1][part]
                lanes = slice(part * half, (part + 1) * half)
                st[i, 0, rows, lanes] = (a + b).astype(BF16)
                st[i, 1, rows, lanes] = (a - b).astype(BF16)
            emit(rows, out)

    def combine(z):
        send_image(z).wait_recv()
        send_shared(z).wait_recv()
        total = acc[lax.rem(z, 2), f] + accr[z].astype(F32)
        total += shq[z, f, 0].astype(F32) * shr[z, 0].astype(F32)
        total += shq[z, f, 1].astype(F32) * shr[z, 1].astype(F32)
        mine = lax.div(z, levels) == d

        @pl.when(mine)
        def _():
            chip[lax.rem(z, levels)] = total

        @pl.when(jnp.logical_not(mine))
        def _():
            xsend[lax.rem(z, levels)] = total.astype(BF16)
            send_section(z).start()

    def place(z):
        j = lax.rem(z, levels)
        send_section(z).wait_recv()
        total = (chip[j] + xrecv[j].astype(F32)).astype(BF16)
        columns = lax.broadcasted_iota(jnp.int32, (TILE, points), 0)
        places = lax.broadcasted_iota(jnp.int32, (TILE, points), 1)
        for owner in range(shots):
            chosen = places == columns + (owner * TILE - start[0])
            chosen = jnp.where(chosen, 1.0, 0.0).astype(BF16)
            zsend[j, owner] = dot(chosen, total).astype(BF16)
        for step in range(1, shots):
            send_columns(j, step).start()

    def one_level(z, carry):
        mine = lax.div(z, levels) == d

        @pl.when(jnp.logical_not(mine))
        def _():
            send_mean(z).wait_recv()

        mean = s0[z][0:1, :]
        turn_shared = om[0:1, :]
        transform(2)
        propagator(1, jnp.square(turn_shared * mean), sign)
        transform(0)
        transform(1)
        propagator(0, jnp.square(turn_own * mean), 1.0)
        advance(2, 1, 1)
        back(2)
        advance(0, 0, -1)
        advance(1, 0, 1)

        @pl.when(jnp.logical_not(mine))
        def _():
            send_slow(z).wait_recv()

        @pl.when(z >= 1)
        def _():
            combine(z - 1)

        def emit_shared(rows, out):
            for side in range(2):
                for part in range(2):
                    shq[z, side, part, rows, :] = out[side][part].astype(BF16)

        def emit_first(rows, out):
            for side in range(2):
                for part in range(2):
                    uq[side, part, rows, :] = out[side][part]

        def emit_second(rows, out):
            for side in range(2):
                product = uq[side, 0, rows, :] * out[side][0] + uq[side, 1, rows, :] * out[side][1]
                acc[lax.rem(z, 2), side, rows, :] = product
                accb[z, side, rows, :] = product.astype(BF16)

        correction(1, sign * turn_shared, ds.at[z])
        finish(2, 1, 1, emit_shared)
        send_shared(z).start()
        correction(0, turn_own, ds.at[z])
        back(0)
        back(1)
        finish(0, 0, -1, emit_first)
        finish(1, 0, 1, emit_second)
        send_image(z).start()

        @pl.when(jnp.logical_and(z >= 1, lax.div(z - 1, levels) == d))
        def _():
            place(z - 1)

        return carry

    lax.fori_loop(0, total_levels, one_level, 0)
    last = total_levels - 1
    combine(last)

    @pl.when(lax.div(last, levels) == d)
    def _():
        place(last)

    for j in range(levels):
        total = zsend[j, s].astype(F32)
        for step in range(1, shots):
            recv_columns(j, step).wait_recv()
            total += zrecv[j, lax.rem(s + step, shots)].astype(F32)
        image[:, j, :] = total

    @pl.when(provider)
    def _():
        send_turn().wait_send()
        send_field().wait_send()

    for j in range(levels):
        send_mean(d * levels + j).wait_send()
        send_slow(d * levels + j).wait_send()
        send_section((1 - d) * levels + j).wait_send()
        for step in range(1, shots):
            send_columns(j, step).wait_send()
    for z in range(total_levels):
        send_image(z).wait_send()
        send_shared(z).wait_send()


def migrate(source, receiver, slowness, omegas, shot_start):
    points = source.shape[-1]
    fronts = source.shape[1]
    levels = slowness.shape[1]
    shots = lax.axis_size("shot")
    total = 2 * levels
    half = points // 2
    full = (points, points)
    side = (points, half)
    vmem, sem = pltpu.VMEM, pltpu.SemaphoreType.DMA
    in_vmem = pl.BlockSpec(memory_space=pltpu.VMEM)
    in_smem = pl.BlockSpec(memory_space=pltpu.SMEM)
    anywhere = pl.BlockSpec(memory_space=pl.ANY)
    return pl.pallas_call(
        functools.partial(migrate_kernel, (points, levels, shots, fronts)),
        out_shape=jax.ShapeDtypeStruct((TILE, levels, half), F32),
        in_specs=[anywhere, anywhere, anywhere, in_smem, in_smem],
        out_specs=in_vmem,
        scratch_shapes=[
            vmem((2, 2) + full, BF16),
            vmem((levels,) + full, F32),
            vmem(full, F32),
            vmem(full, F32),
            vmem((3, 2) + full, F32),
            vmem((3, 2) + full, F32),
            vmem((3, 2) + full, BF16),
            vmem((total,) + full, BF16),
            vmem((total, 8, points), F32),
            vmem((8, points), F32),
            vmem((2,) + full, F32),
            vmem((2,) + full, F32),
            vmem((2,) + full, F32),
            vmem((2,) + full, F32),
            vmem((3, 2) + full, BF16),
            vmem((3, 2) + full, BF16),
            vmem((3, 2) + full, BF16),
            vmem((2, 2) + side, F32),
            vmem((2, 2) + side, F32),
            vmem((total, 2) + side, BF16),
            vmem((total, 2, 2) + side, BF16),
            vmem((total,) + side, BF16),
            vmem((total, 2) + side, BF16),
            vmem((levels,) + side, F32),
            vmem((levels,) + side, BF16),
            vmem((levels,) + side, BF16),
            vmem((levels, shots, TILE, half), BF16),
            vmem((levels, shots, TILE, half), BF16),
            sem((3,)),
            sem((levels,)),
            sem((2, total)),
            sem((2, total)),
            sem((2, 1)),
            sem((2, 1)),
            sem((2, total)),
            sem((2, total)),
            sem((2, levels)),
            sem((levels, shots)),
            sem((levels, shots)),
        ],
        compiler_params=pltpu.CompilerParams(
            collective_id=0, has_side_effects=True, vmem_limit_bytes=60 * 1024 * 1024
        ),
        name="migrate",
    )(source, receiver, slowness, omegas, shot_start)


def solution(mesh):
    sizes = mesh.shape

    def per_device(source, *rest):
        if sizes["depth"] == 2 and sizes["freq"] == 2 and source.shape[1] == 3:
            return migrate(source, *rest)
        return local(source, *rest)

    return jax.shard_map(
        per_device,
        mesh=mesh,
        in_specs=(
            P(("groups", "shot"), "freq", None, None, None),
            P(("groups", "shot"), "freq", None, None, None),
            P(("groups", "shot"), "depth", None, None),
            P(("groups", "shot"), "freq"),
            P(("groups", "shot")),
        ),
        out_specs=P(("groups", "shot"), "depth", "freq"),
        check_vma=False,
    )
```

```python
import functools

import jax
import jax.numpy as jnp
import numpy as np
from jax import lax
from jax.experimental import pallas as pl
from jax.experimental.pallas import tpu as pltpu
from jax.sharding import PartitionSpec as P

TILE = 128


def from_behind(array, axis, by):
    peers = lax.axis_size(axis)
    pairs = [(i, i + by) for i in range(peers) if 0 <= i + by < peers]
    return lax.ppermute(array, axis, pairs)


def tables(points):
    positions = jnp.arange(points, dtype=jnp.int32)
    product = positions[:, None] * positions[None, :] % points
    angles = 2.0 * jnp.pi / points * product.astype(jnp.float32)
    cosine_table = jnp.cos(angles).astype(jnp.bfloat16)
    sine_table = jnp.sin(angles).astype(jnp.bfloat16)
    forward = jnp.concatenate(
        [
            jnp.concatenate([cosine_table, -sine_table], axis=1),
            jnp.concatenate([sine_table, cosine_table], axis=1),
        ],
        axis=0,
    )
    inverse = jnp.concatenate(
        [
            jnp.concatenate([cosine_table, sine_table], axis=1),
            jnp.concatenate([-sine_table, cosine_table], axis=1),
        ],
        axis=0,
    )
    return (forward, inverse)


def lateral_grids(points):
    positions = jnp.arange(points, dtype=jnp.int32)
    wrapped = (positions + points // 2) % points - points // 2
    wavenumber = 2.0 * jnp.pi / points * wrapped.astype(jnp.float32)
    edge_width = points // 16
    distance_in = jnp.minimum(positions, points - 1 - positions) + 1
    edge_taper = jnp.minimum(distance_in.astype(jnp.float32) / edge_width, 1.0)
    return (wavenumber, edge_taper)


def flip_parts(field_in):
    leading = field_in.shape[:-2]
    row_count = field_in.shape[-2]
    col_count = field_in.shape[-1] // 2
    pieces = field_in.reshape(leading + (row_count, 2, col_count))
    moved = jnp.swapaxes(pieces, -3, -1)
    return moved.reshape(leading + (col_count, 2 * row_count))


def extrapolate(
    wave_state, slow_level, angular, field_signs, forward, inverse, wavenumber, edge_taper
):
    batch_size, points, width = wave_state.shape
    inv_points = 1.0 / points
    half_done = jnp.dot(
        wave_state.reshape(batch_size * points, width), forward, preferred_element_type=jnp.float32
    )
    half_done = flip_parts(half_done.astype(jnp.bfloat16).reshape(batch_size, points, width))
    spectrum = jnp.dot(
        half_done.reshape(batch_size * points, width), forward, preferred_element_type=jnp.float32
    ).reshape(batch_size, points, width)
    mean_slow = jnp.mean(slow_level)
    radius_sq = jnp.square(angular * mean_slow)
    square = jnp.square(wavenumber)[:, None] + jnp.square(wavenumber)[None, :]
    vertical = radius_sq[:, None, None] - square[None]
    real_kz = jnp.sqrt(jnp.maximum(vertical, 0.0))
    damping = jnp.exp(-jnp.sqrt(jnp.maximum(-vertical, 0.0)))
    phase_turn = field_signs[:, None, None] * real_kz
    phase_real = damping * jnp.cos(phase_turn)
    phase_imag = damping * jnp.sin(phase_turn)
    spec_real = spectrum[..., :points]
    spec_imag = spectrum[..., points:]
    shifted = jnp.concatenate(
        [
            spec_real * phase_real - spec_imag * phase_imag,
            spec_real * phase_imag + spec_imag * phase_real,
        ],
        axis=-1,
    ).astype(jnp.bfloat16)
    half_back = (
        jnp.dot(
            shifted.reshape(batch_size * points, width), inverse, preferred_element_type=jnp.float32
        )
        * inv_points
    )
    half_back = flip_parts(half_back.astype(jnp.bfloat16).reshape(batch_size, points, width))
    field_out = (
        jnp.dot(
            half_back.reshape(batch_size * points, width),
            inverse,
            preferred_element_type=jnp.float32,
        ).reshape(batch_size, points, width)
        * inv_points
    )
    correction = (field_signs * angular)[:, None, None] * (slow_level - mean_slow)[None]
    window = edge_taper[:, None] * edge_taper[None, :]
    corr_real = jnp.cos(correction) * window[None]
    corr_imag = jnp.sin(correction) * window[None]
    field_real = field_out[..., :points]
    field_imag = field_out[..., points:]
    return (
        field_real * corr_real - field_imag * corr_imag,
        field_real * corr_imag + field_imag * corr_real,
    )


def local(source, receiver, slowness, omegas, shot_start):
    points = source.shape[-1]
    fronts = source.shape[1]
    levels = slowness.shape[1]
    segments = lax.axis_size("depth")
    segment_index = lax.axis_index("depth")
    forward, inverse = tables(points)
    wavenumber, edge_taper = lateral_grids(points)
    field_signs = jnp.array([-1.0, 1.0], jnp.float32)

    def surface(chosen):
        src_front = lax.dynamic_index_in_dim(source[0], chosen, 0, keepdims=False)
        rcv_front = lax.dynamic_index_in_dim(receiver[0], chosen, 0, keepdims=False)
        paired = jnp.stack([src_front, rcv_front])
        return jnp.concatenate([paired[:, 0], paired[:, 1]], axis=-1).astype(jnp.bfloat16)

    def extrapolate_front(operands):
        wave_state, rate_now = operands
        angular = jnp.stack([rate_now, rate_now])
        level_terms = []
        for level_index in range(levels):
            real_part, imag_part = extrapolate(
                wave_state,
                slowness[0, level_index],
                angular,
                field_signs,
                forward,
                inverse,
                wavenumber,
                edge_taper,
            )
            level_terms.append(real_part[0] * real_part[1] + imag_part[0] * imag_part[1])
            wave_state = jnp.concatenate([real_part, imag_part], axis=-1).astype(jnp.bfloat16)
        return (wave_state, jnp.stack(level_terms, axis=1))

    def stay_still(operands):
        wave_state, rate_now = operands
        return (jnp.zeros_like(wave_state), jnp.zeros((points, levels, points), jnp.float32))

    def one_turn(turn_index, carry):
        incoming, image_sum = carry
        front_index = turn_index - segment_index
        active = jnp.logical_and(front_index >= 0, front_index < fronts)
        chosen = jnp.clip(front_index, 0, fronts - 1)
        begin_field = jnp.where(segment_index == 0, surface(chosen), incoming)
        rate_now = lax.dynamic_index_in_dim(omegas[0], chosen, 0, keepdims=False)
        wave_state, level_image = lax.cond(
            active, extrapolate_front, stay_still, (begin_field, rate_now)
        )
        incoming = from_behind(wave_state, "depth", 1)
        return (incoming, image_sum + level_image)

    initial = (
        jnp.zeros((2, points, 2 * points), jnp.bfloat16),
        jnp.zeros((points, levels, points), jnp.float32),
    )
    final_carry = lax.fori_loop(0, segments + fronts - 1, one_turn, initial)
    local_image = lax.psum_scatter(
        final_carry[1].astype(jnp.bfloat16), "freq", scatter_dimension=2, tiled=True
    ).astype(jnp.float32)
    aperture_start = shot_start[0]
    owners = lax.axis_size("shot")
    survey_cols = owners * TILE
    padding = jnp.zeros((survey_cols,) + local_image.shape[1:], jnp.float32)
    padded = jnp.concatenate([padding, local_image, padding], axis=0)
    offset = jnp.clip(
        jnp.zeros((), jnp.int32) - aperture_start + survey_cols, 0, points + survey_cols
    )
    placed = lax.dynamic_slice_in_dim(padded, offset, survey_cols, 0)
    blocks = placed.reshape((owners, TILE) + local_image.shape[1:])
    received = lax.all_to_all(
        blocks.astype(jnp.bfloat16), "shot", split_axis=0, concat_axis=0, tiled=True
    ).astype(blocks.dtype)
    collected = jnp.sum(received, axis=0)
    return collected


MESH = pl.DeviceIdType.MESH
BF16 = jnp.bfloat16
CHUNK = 32
F32 = jnp.float32
SLOWEST, SLOWNESS_SPAN, FASTEST_TURN = 1.4, 0.8, 2.5


def even_polynomial(function, limit, degree):
    series = np.polynomial.chebyshev.Chebyshev.interpolate(
        lambda x: function(np.sqrt(np.maximum(x, 0.0))), degree, domain=[0.0, limit]
    )
    return [float(c) for c in series.convert(kind=np.polynomial.Polynomial).coef]


def horner(coefficients, x):
    total = coefficients[-1] * x + coefficients[-2]
    for c in coefficients[-3::-1]:
        total = total * x + c
    return total


def sinc(y):
    return np.sinc(y / np.pi)


def migrate_kernel(
    dims, source, receiver, slowness, omegas, start, image,
    tab, slow, square, window, res, fbuf, st, ds, s0, om, pr, pi, cr, ci, bb, ww, xx, uq, acc, accb, shq, accr, shr, chip,
    xsend, xrecv, zsend, zrecv,
    load_sem, slow_sem, ds_sem, s0_sem, sh_sem, om_sem, acc_sem, shq_sem, x_sem, zs_sem, zr_sem,
):
    points, levels, shots, fronts = dims
    half, quarter = points // 2, points // 4
    total_levels = 2 * levels
    d, f, s = lax.axis_index("depth"), lax.axis_index("freq"), lax.axis_index("shot")
    other_core, other_chip = {"freq": 1 - f}, {"depth": 1 - d}
    provider = f == d

    barrier = pltpu.get_barrier_semaphore()
    pl.semaphore_signal(barrier, inc=1, device_id=other_core, device_id_type=MESH)
    pl.semaphore_signal(barrier, inc=1, device_id=other_chip, device_id_type=MESH)
    for step in range(1, shots):
        pl.semaphore_signal(
            barrier, inc=1, device_id={"shot": lax.rem(s + step, shots)}, device_id_type=MESH
        )

    def load(index, front, field):
        return pltpu.make_async_copy(field.at[0, front], fbuf.at[index], load_sem.at[index])

    def remote(source_ref, target_ref, sems, device, index):
        return pltpu.make_async_remote_copy(
            src_ref=source_ref, dst_ref=target_ref, send_sem=sems.at[0, index],
            recv_sem=sems.at[1, index], device_id=device, device_id_type=MESH,
        )

    def send_field():
        return send_front(source)

    def send_front(field):
        return remote(field.at[0, fronts - 1], fbuf.at[2], sh_sem, other_core, 0)

    def load_slow(j):
        return pltpu.make_async_copy(slowness.at[0, j], slow.at[j], slow_sem.at[j])

    def send_turn():
        return remote(om, om, om_sem, other_core, 0)

    def send_slow(z):
        return remote(ds.at[z], ds.at[z], ds_sem, other_chip, z)

    def send_mean(z):
        return remote(s0.at[z], s0.at[z], s0_sem, other_chip, z)

    def send_image(z):
        return remote(accb.at[z, 1 - f], accr.at[z], acc_sem, other_core, z)

    def send_shared(z):
        return remote(shq.at[z, 1 - f], shr.at[z], shq_sem, other_core, z)

    def send_section(z):
        j = lax.rem(z, levels)
        return remote(xsend.at[j], xrecv.at[j], x_sem, other_chip, j)

    def send_columns(j, step):
        owner = lax.rem(s + step, shots)
        return pltpu.make_async_remote_copy(
            src_ref=zsend.at[j, owner], dst_ref=zrecv.at[j, s], send_sem=zs_sem.at[j, owner],
            recv_sem=zr_sem.at[j, s], device_id={"shot": owner}, device_id_type=MESH,
        )

    def recv_columns(j, step):
        owner = lax.rem(s + step, shots)
        return pltpu.make_async_remote_copy(
            src_ref=zsend.at[j, owner], dst_ref=zrecv.at[j, owner], send_sem=zs_sem.at[j, owner],
            recv_sem=zr_sem.at[j, owner], device_id={"shot": owner}, device_id_type=MESH,
        )

    for j in range(levels):
        load_slow(j).start()
    for front in range(2):
        @pl.when(jnp.logical_and(provider, f == front))
        def _(field=(source, receiver)[front]):
            load(2, fronts - 1, field).start()

    load(0, d, source).start()
    load(1, d, receiver).start()

    def grid_index(axis):
        at = lax.broadcasted_iota(jnp.int32, (points, points), axis)
        odd = jnp.where(at >= half, 1, 0)
        wave = 2 * jnp.where(at - half * odd >= quarter, at - half * odd - quarter, at - half * odd)
        return at, jnp.where(at == quarter, half, wave + odd).astype(F32) * (2.0 * np.pi / points)

    row, row_wave = grid_index(0)
    column, column_wave = grid_index(1)
    square[...] = jnp.square(row_wave) + jnp.square(column_wave)

    table_cos = even_polynomial(np.cos, np.pi**2, 8)
    table_sinc = even_polynomial(sinc, np.pi**2, 8)

    def frequency(axis, part):
        at = lax.broadcasted_iota(jnp.int32, (half, half), axis)
        if part == 1:
            return jnp.where(at < quarter, 2 * at + 1, points - 1 - 2 * (at - quarter))
        mirrored = jnp.where(at == quarter, half, points - 2 * (at - quarter))
        return jnp.where(at < quarter, 2 * at, mirrored)

    for part in range(2):
        for turned in range(2):
            place = lax.broadcasted_iota(jnp.int32, (half, half), turned)
            product = place * frequency(1 - turned, part)
            wrapped = ((product + half) & (points - 1)) - half
            x = wrapped.astype(F32) * (2.0 * np.pi / points)
            cosine = horner(table_cos, x * x).astype(BF16)
            sine = x * horner(table_sinc, x * x)
            upper, lower = ((-sine).astype(BF16), sine.astype(BF16))
            if turned:
                upper, lower = lower, upper
            tab[turned, part, :half, :half] = cosine
            tab[turned, part, half:, half:] = cosine
            tab[turned, part, :half, half:] = upper
            tab[turned, part, half:, :half] = lower

    def taper(at):
        distance_in = (jnp.minimum(at, points - 1 - at) + 1).astype(F32)
        return jnp.minimum(distance_in * (16.0 / points), 1.0)

    window[...] = taper(row) * taper(column) * (1.0 / points)

    pl.semaphore_wait(barrier, shots + 1)
    for front in range(2):
        @pl.when(jnp.logical_and(provider, f == front))
        def _(field=(receiver, source)[front]):
            om[...] = jnp.full((8, points), omegas[0, fronts - 1], F32)
            send_turn().start()
            send_front(field).start()

    for j in range(levels):
        load_slow(j).wait()
        mean = jnp.mean(slow[j])
        ds[d * levels + j] = (slow[j] - mean).astype(BF16)
        s0[d * levels + j] = jnp.full((8, points), mean, F32)
        send_mean(d * levels + j).start()
        send_slow(d * levels + j).start()

    def fold_into(slot, re, im):
        lo, hi = slice(0, half), slice(half, points)
        for at in range(0, points, CHUNK):
            rows, into = slice(at, at + CHUNK), slice(slot * points + at, slot * points + at + CHUNK)
            for lanes, x in ((lo, re), (hi, im)):
                a, b = x[rows, lo], x[rows, hi]
                st[0, into, lanes] = (a + b).astype(BF16)
                st[1, into, lanes] = (a - b).astype(BF16)

    for index, field in enumerate((source, receiver)):
        load(index, d, field).wait()
        fold_into(index, fbuf.at[index, 0], fbuf.at[index, 1])

    @pl.when(provider)
    def _():
        load(2, fronts - 1, source).wait()

    @pl.when(jnp.logical_not(provider))
    def _():
        send_turn().wait_recv()
        send_field().wait_recv()

    fold_into(2, fbuf.at[2, 0], fbuf.at[2, 1])

    turn_own = omegas[0, d]
    sign = (2 * f - 1).astype(F32)
    limit = 1.01 * (FASTEST_TURN * SLOWEST) ** 2
    kz_cos = even_polynomial(np.cos, limit, 5)
    kz_sinc = even_polynomial(sinc, limit, 5)
    limit = 1.01 * (FASTEST_TURN * SLOWNESS_SPAN) ** 2
    turn_cos = even_polynomial(np.cos, limit, 4)
    turn_sinc = even_polynomial(sinc, limit, 3)
    inv = 1.0 / points

    def propagator(index, radius_sq, flip):
        def rows(at, count, targets):
            vertical = radius_sq - square[at : at + count, :]
            size = jnp.abs(vertical)
            root = size * lax.rsqrt(jnp.maximum(size, 1e-30))
            positive = vertical >= 0.0
            x = jnp.maximum(vertical, 0.0)
            re = jnp.where(positive, horner(kz_cos, x), jnp.exp(-root)) * inv
            im = jnp.where(positive, root * horner(kz_sinc, x), 0.0) * (inv * flip)
            for target in targets:
                pr[index, target : target + count, :] = re
                pi[index, target : target + count, :] = im

        step = quarter // 2
        for at in range(0, quarter, step):
            rows(at, step, (at, at + quarter))
            rows(half + at, step, (half + at, half + quarter + at))
        rows(quarter, 8, (quarter,))

    def correction(index, turn, slow):
        step = quarter // 2
        for at in range(0, points, step):
            x = turn * slow[at : at + step, :].astype(F32)
            y = x * x
            w = window[at : at + step, :]
            cr[index, at : at + step, :] = horner(turn_cos, y) * w
            ci[index, at : at + step, :] = horner(turn_sinc, y) * (x * w)

    def dot(a, b):
        return jnp.dot(a, b, preferred_element_type=F32)

    def transform_all():
        for part in range(2):
            res[part] = dot(st[part], tab[0, part])
        for i in range(3):
            for part in range(2):
                lanes = slice(part * half, (part + 1) * half)
                for at in range(0, half, CHUNK):
                    row = i * points + at
                    top = res[part, row : row + CHUNK, :]
                    bottom = res[part, half + row : half + row + CHUNK, :]
                    for fold, w in ((0, top + bottom), (1, top - bottom)):
                        bb[i, fold, at : at + CHUNK, lanes] = w[:, :half].astype(BF16)
                        bb[i, fold, half + at : half + at + CHUNK, lanes] = w[:, half:].astype(BF16)

    def advance(i, which, sigma):
        for part in range(2):
            base = i * points
            res[part, base : base + points, :] = dot(tab[1, part], bb[i, part])
            for at in range(0, half, CHUNK):
                rows = slice(part * half + at, part * half + at + CHUNK)
                top, bottom = slice(at, at + CHUNK), slice(half + at, half + at + CHUNK)
                re = res[part, base + at : base + at + CHUNK, :]
                im = res[part, base + half + at : base + half + at + CHUNK, :]
                p, q = pr[which, rows, :], pi[which, rows, :]
                if sigma > 0:
                    ww[i, part, top, :] = (re * p - im * q).astype(BF16)
                    ww[i, part, bottom, :] = (re * q + im * p).astype(BF16)
                else:
                    ww[i, part, top, :] = (re * p + im * q).astype(BF16)
                    ww[i, part, bottom, :] = (im * p - re * q).astype(BF16)

    def back(i):
        for part in range(2):
            res[part, i * points : (i + 1) * points, :] = dot(tab[0, part], ww[i, part])
        for at in range(0, points, CHUNK):
            rows = slice(i * points + at, i * points + at + CHUNK)
            even, odd = res[0, rows, :], res[1, rows, :]
            target = at % half
            lanes = slice(0, half) if at < half else slice(half, points)
            for start_row, y in ((0, even + odd), (half, even - odd)):
                into = slice(start_row + target, start_row + target + CHUNK)
                xx[i, 0, into, lanes] = y[:, :half].astype(BF16)
                xx[i, 1, into, lanes] = y[:, half:].astype(BF16)

    def finish(i, which, sigma, emit):
        for part in range(2):
            res[part, i * points : (i + 1) * points, :] = dot(xx[i, part], tab[1, part])
        for at in range(0, points, CHUNK):
            rows = slice(at, at + CHUNK)
            into = slice(i * points + at, i * points + at + CHUNK)
            even, odd = res[0, into, :], res[1, into, :]
            out = []
            for lanes, y in ((slice(0, half), even + odd), (slice(half, points), even - odd)):
                re, im = y[:, :half], y[:, half:]
                c, t = cr[which, rows, lanes], ci[which, rows, lanes]
                if sigma > 0:
                    out.append((re * c - im * t, re * t + im * c))
                else:
                    out.append((re * c + im * t, im * c - re * t))
            for part in range(2):
                a, b = out[0][part], out[1][part]
                lanes = slice(part * half, (part + 1) * half)
                st[0, into, lanes] = (a + b).astype(BF16)
                st[1, into, lanes] = (a - b).astype(BF16)
            emit(rows, out)

    def combine(z):
        send_image(z).wait_recv()
        send_shared(z).wait_recv()
        total = acc[lax.rem(z, 2), f] + accr[z].astype(F32)
        total += shq[z, f, 0].astype(F32) * shr[z, 0].astype(F32)
        total += shq[z, f, 1].astype(F32) * shr[z, 1].astype(F32)
        mine = lax.div(z, levels) == d

        @pl.when(mine)
        def _():
            chip[lax.rem(z, levels)] = total

        @pl.when(jnp.logical_not(mine))
        def _():
            xsend[lax.rem(z, levels)] = total.astype(BF16)
            send_section(z).start()

    def place(z):
        j = lax.rem(z, levels)
        send_section(z).wait_recv()
        total = (chip[j] + xrecv[j].astype(F32)).astype(BF16)
        columns = lax.broadcasted_iota(jnp.int32, (TILE, points), 0)
        places = lax.broadcasted_iota(jnp.int32, (TILE, points), 1)
        for owner in range(shots):
            chosen = places == columns + (owner * TILE - start[0])
            chosen = jnp.where(chosen, 1.0, 0.0).astype(BF16)
            zsend[j, owner] = dot(chosen, total).astype(BF16)
        for step in range(1, shots):
            send_columns(j, step).start()

    def one_level(z, carry):
        mine = lax.div(z, levels) == d

        @pl.when(jnp.logical_not(mine))
        def _():
            send_mean(z).wait_recv()

        mean = s0[z][0:1, :]
        turn_shared = om[0:1, :]
        transform_all()
        propagator(1, jnp.square(turn_shared * mean), sign)
        propagator(0, jnp.square(turn_own * mean), 1.0)
        advance(2, 1, 1)
        back(2)
        advance(0, 0, -1)
        advance(1, 0, 1)

        @pl.when(jnp.logical_not(mine))
        def _():
            send_slow(z).wait_recv()

        @pl.when(z >= 1)
        def _():
            combine(z - 1)

        def emit_shared(rows, out):
            for side in range(2):
                for part in range(2):
                    shq[z, side, part, rows, :] = out[side][part].astype(BF16)

        def emit_first(rows, out):
            for side in range(2):
                for part in range(2):
                    uq[side, part, rows, :] = out[side][part]

        def emit_second(rows, out):
            for side in range(2):
                product = uq[side, 0, rows, :] * out[side][0] + uq[side, 1, rows, :] * out[side][1]
                acc[lax.rem(z, 2), side, rows, :] = product
                accb[z, side, rows, :] = product.astype(BF16)

        correction(1, sign * turn_shared, ds.at[z])
        finish(2, 1, 1, emit_shared)
        send_shared(z).start()
        correction(0, turn_own, ds.at[z])
        back(0)
        back(1)
        finish(0, 0, -1, emit_first)
        finish(1, 0, 1, emit_second)
        send_image(z).start()

        before = z - 2 + d

        @pl.when(jnp.logical_and(before >= d * levels, before < (d + 1) * levels))
        def _():
            place(before)

        return carry

    lax.fori_loop(0, total_levels, one_level, 0)
    last = total_levels - 1
    combine(last)

    @pl.when(lax.div(last, levels) == d)
    def _():
        place(last)

    for j in range(levels):
        total = zsend[j, s].astype(F32)
        for step in range(1, shots):
            recv_columns(j, step).wait_recv()
            total += zrecv[j, lax.rem(s + step, shots)].astype(F32)
        image[pl.ds(j, TILE, stride=levels), :] = total

    @pl.when(provider)
    def _():
        send_turn().wait_send()
        send_field().wait_send()

    for j in range(levels):
        send_mean(d * levels + j).wait_send()
        send_slow(d * levels + j).wait_send()
        send_section((1 - d) * levels + j).wait_send()
        for step in range(1, shots):
            send_columns(j, step).wait_send()
    for z in range(total_levels):
        send_image(z).wait_send()
        send_shared(z).wait_send()


def migrate(source, receiver, slowness, omegas, shot_start):
    points = source.shape[-1]
    fronts = source.shape[1]
    levels = slowness.shape[1]
    shots = lax.axis_size("shot")
    total = 2 * levels
    half = points // 2
    full = (points, points)
    side = (points, half)
    vmem, sem = pltpu.VMEM, pltpu.SemaphoreType.DMA
    in_vmem = pl.BlockSpec(memory_space=pltpu.VMEM)
    in_smem = pl.BlockSpec(memory_space=pltpu.SMEM)
    anywhere = pl.BlockSpec(memory_space=pl.ANY)
    return pl.pallas_call(
        functools.partial(migrate_kernel, (points, levels, shots, fronts)),
        out_shape=jax.ShapeDtypeStruct((TILE * levels, half), F32),
        in_specs=[anywhere, anywhere, anywhere, in_smem, in_smem],
        out_specs=in_vmem,
        scratch_shapes=[
            vmem((2, 2) + full, BF16),
            vmem((levels,) + full, F32),
            vmem(full, F32),
            vmem(full, F32),
            vmem((2, 3 * points, points), F32),
            vmem((3, 2) + full, F32),
            vmem((2, 3 * points, points), BF16),
            vmem((total,) + full, BF16),
            vmem((total, 8, points), F32),
            vmem((8, points), F32),
            vmem((2,) + full, F32),
            vmem((2,) + full, F32),
            vmem((2,) + full, F32),
            vmem((2,) + full, F32),
            vmem((3, 2) + full, BF16),
            vmem((3, 2) + full, BF16),
            vmem((3, 2) + full, BF16),
            vmem((2, 2) + side, F32),
            vmem((2, 2) + side, F32),
            vmem((total, 2) + side, BF16),
            vmem((total, 2, 2) + side, BF16),
            vmem((total,) + side, BF16),
            vmem((total, 2) + side, BF16),
            vmem((levels,) + side, F32),
            vmem((levels,) + side, BF16),
            vmem((levels,) + side, BF16),
            vmem((levels, shots, TILE, half), BF16),
            vmem((levels, shots, TILE, half), BF16),
            sem((3,)),
            sem((levels,)),
            sem((2, total)),
            sem((2, total)),
            sem((2, 1)),
            sem((2, 1)),
            sem((2, total)),
            sem((2, total)),
            sem((2, levels)),
            sem((levels, shots)),
            sem((levels, shots)),
        ],
        compiler_params=pltpu.CompilerParams(
            collective_id=0, has_side_effects=True, vmem_limit_bytes=60 * 1024 * 1024
        ),
        name="migrate",
    )(source, receiver, slowness, omegas, shot_start).reshape(TILE, levels, half)


def solution(mesh):
    sizes = mesh.shape

    def per_device(source, receiver, slowness, *rest):
        if sizes["depth"] == 2 and sizes["freq"] == 2 and source.shape[1] == 3 and slowness.shape[1] > 1:
            return migrate(source, receiver, slowness, *rest)
        return local(source, receiver, slowness, *rest)

    return jax.shard_map(
        per_device,
        mesh=mesh,
        in_specs=(
            P(("groups", "shot"), "freq", None, None, None),
            P(("groups", "shot"), "freq", None, None, None),
            P(("groups", "shot"), "depth", None, None),
            P(("groups", "shot"), "freq"),
            P(("groups", "shot")),
        ),
        out_specs=P(("groups", "shot"), "depth", "freq"),
        check_vma=False,
    )
```

```python
import functools

import jax
import jax.numpy as jnp
import numpy as np
from jax import lax
from jax.experimental import pallas as pl
from jax.experimental.pallas import tpu as pltpu
from jax.sharding import PartitionSpec as P

TILE = 128


def from_behind(array, axis, by):
    peers = lax.axis_size(axis)
    pairs = [(i, i + by) for i in range(peers) if 0 <= i + by < peers]
    return lax.ppermute(array, axis, pairs)


def tables(points):
    positions = jnp.arange(points, dtype=jnp.int32)
    product = positions[:, None] * positions[None, :] % points
    angles = 2.0 * jnp.pi / points * product.astype(jnp.float32)
    cosine_table = jnp.cos(angles).astype(jnp.bfloat16)
    sine_table = jnp.sin(angles).astype(jnp.bfloat16)
    forward = jnp.concatenate(
        [
            jnp.concatenate([cosine_table, -sine_table], axis=1),
            jnp.concatenate([sine_table, cosine_table], axis=1),
        ],
        axis=0,
    )
    inverse = jnp.concatenate(
        [
            jnp.concatenate([cosine_table, sine_table], axis=1),
            jnp.concatenate([-sine_table, cosine_table], axis=1),
        ],
        axis=0,
    )
    return (forward, inverse)


def lateral_grids(points):
    positions = jnp.arange(points, dtype=jnp.int32)
    wrapped = (positions + points // 2) % points - points // 2
    wavenumber = 2.0 * jnp.pi / points * wrapped.astype(jnp.float32)
    edge_width = points // 16
    distance_in = jnp.minimum(positions, points - 1 - positions) + 1
    edge_taper = jnp.minimum(distance_in.astype(jnp.float32) / edge_width, 1.0)
    return (wavenumber, edge_taper)


def flip_parts(field_in):
    leading = field_in.shape[:-2]
    row_count = field_in.shape[-2]
    col_count = field_in.shape[-1] // 2
    pieces = field_in.reshape(leading + (row_count, 2, col_count))
    moved = jnp.swapaxes(pieces, -3, -1)
    return moved.reshape(leading + (col_count, 2 * row_count))


def extrapolate(
    wave_state, slow_level, angular, field_signs, forward, inverse, wavenumber, edge_taper
):
    batch_size, points, width = wave_state.shape
    inv_points = 1.0 / points
    half_done = jnp.dot(
        wave_state.reshape(batch_size * points, width), forward, preferred_element_type=jnp.float32
    )
    half_done = flip_parts(half_done.astype(jnp.bfloat16).reshape(batch_size, points, width))
    spectrum = jnp.dot(
        half_done.reshape(batch_size * points, width), forward, preferred_element_type=jnp.float32
    ).reshape(batch_size, points, width)
    mean_slow = jnp.mean(slow_level)
    radius_sq = jnp.square(angular * mean_slow)
    square = jnp.square(wavenumber)[:, None] + jnp.square(wavenumber)[None, :]
    vertical = radius_sq[:, None, None] - square[None]
    real_kz = jnp.sqrt(jnp.maximum(vertical, 0.0))
    damping = jnp.exp(-jnp.sqrt(jnp.maximum(-vertical, 0.0)))
    phase_turn = field_signs[:, None, None] * real_kz
    phase_real = damping * jnp.cos(phase_turn)
    phase_imag = damping * jnp.sin(phase_turn)
    spec_real = spectrum[..., :points]
    spec_imag = spectrum[..., points:]
    shifted = jnp.concatenate(
        [
            spec_real * phase_real - spec_imag * phase_imag,
            spec_real * phase_imag + spec_imag * phase_real,
        ],
        axis=-1,
    ).astype(jnp.bfloat16)
    half_back = (
        jnp.dot(
            shifted.reshape(batch_size * points, width), inverse, preferred_element_type=jnp.float32
        )
        * inv_points
    )
    half_back = flip_parts(half_back.astype(jnp.bfloat16).reshape(batch_size, points, width))
    field_out = (
        jnp.dot(
            half_back.reshape(batch_size * points, width),
            inverse,
            preferred_element_type=jnp.float32,
        ).reshape(batch_size, points, width)
        * inv_points
    )
    correction = (field_signs * angular)[:, None, None] * (slow_level - mean_slow)[None]
    window = edge_taper[:, None] * edge_taper[None, :]
    corr_real = jnp.cos(correction) * window[None]
    corr_imag = jnp.sin(correction) * window[None]
    field_real = field_out[..., :points]
    field_imag = field_out[..., points:]
    return (
        field_real * corr_real - field_imag * corr_imag,
        field_real * corr_imag + field_imag * corr_real,
    )


def local(source, receiver, slowness, omegas, shot_start):
    points = source.shape[-1]
    fronts = source.shape[1]
    levels = slowness.shape[1]
    segments = lax.axis_size("depth")
    segment_index = lax.axis_index("depth")
    forward, inverse = tables(points)
    wavenumber, edge_taper = lateral_grids(points)
    field_signs = jnp.array([-1.0, 1.0], jnp.float32)

    def surface(chosen):
        src_front = lax.dynamic_index_in_dim(source[0], chosen, 0, keepdims=False)
        rcv_front = lax.dynamic_index_in_dim(receiver[0], chosen, 0, keepdims=False)
        paired = jnp.stack([src_front, rcv_front])
        return jnp.concatenate([paired[:, 0], paired[:, 1]], axis=-1).astype(jnp.bfloat16)

    def extrapolate_front(operands):
        wave_state, rate_now = operands
        angular = jnp.stack([rate_now, rate_now])
        level_terms = []
        for level_index in range(levels):
            real_part, imag_part = extrapolate(
                wave_state,
                slowness[0, level_index],
                angular,
                field_signs,
                forward,
                inverse,
                wavenumber,
                edge_taper,
            )
            level_terms.append(real_part[0] * real_part[1] + imag_part[0] * imag_part[1])
            wave_state = jnp.concatenate([real_part, imag_part], axis=-1).astype(jnp.bfloat16)
        return (wave_state, jnp.stack(level_terms, axis=1))

    def stay_still(operands):
        wave_state, rate_now = operands
        return (jnp.zeros_like(wave_state), jnp.zeros((points, levels, points), jnp.float32))

    def one_turn(turn_index, carry):
        incoming, image_sum = carry
        front_index = turn_index - segment_index
        active = jnp.logical_and(front_index >= 0, front_index < fronts)
        chosen = jnp.clip(front_index, 0, fronts - 1)
        begin_field = jnp.where(segment_index == 0, surface(chosen), incoming)
        rate_now = lax.dynamic_index_in_dim(omegas[0], chosen, 0, keepdims=False)
        wave_state, level_image = lax.cond(
            active, extrapolate_front, stay_still, (begin_field, rate_now)
        )
        incoming = from_behind(wave_state, "depth", 1)
        return (incoming, image_sum + level_image)

    initial = (
        jnp.zeros((2, points, 2 * points), jnp.bfloat16),
        jnp.zeros((points, levels, points), jnp.float32),
    )
    final_carry = lax.fori_loop(0, segments + fronts - 1, one_turn, initial)
    local_image = lax.psum_scatter(
        final_carry[1].astype(jnp.bfloat16), "freq", scatter_dimension=2, tiled=True
    ).astype(jnp.float32)
    aperture_start = shot_start[0]
    owners = lax.axis_size("shot")
    survey_cols = owners * TILE
    padding = jnp.zeros((survey_cols,) + local_image.shape[1:], jnp.float32)
    padded = jnp.concatenate([padding, local_image, padding], axis=0)
    offset = jnp.clip(
        jnp.zeros((), jnp.int32) - aperture_start + survey_cols, 0, points + survey_cols
    )
    placed = lax.dynamic_slice_in_dim(padded, offset, survey_cols, 0)
    blocks = placed.reshape((owners, TILE) + local_image.shape[1:])
    received = lax.all_to_all(
        blocks.astype(jnp.bfloat16), "shot", split_axis=0, concat_axis=0, tiled=True
    ).astype(blocks.dtype)
    collected = jnp.sum(received, axis=0)
    return collected


MESH = pl.DeviceIdType.MESH
BF16 = jnp.bfloat16
CHUNK = 32
F32 = jnp.float32
SLOWEST, SLOWNESS_SPAN, FASTEST_TURN = 1.4, 0.8, 2.5


def even_polynomial(function, limit, degree):
    series = np.polynomial.chebyshev.Chebyshev.interpolate(
        lambda x: function(np.sqrt(np.maximum(x, 0.0))), degree, domain=[0.0, limit]
    )
    return [float(c) for c in series.convert(kind=np.polynomial.Polynomial).coef]


def horner(coefficients, x):
    total = coefficients[-1] * x + coefficients[-2]
    for c in coefficients[-3::-1]:
        total = total * x + c
    return total


def sinc(y):
    return np.sinc(y / np.pi)


def migrate_kernel(
    dims, source, receiver, slowness, omegas, start, image,
    tab, slow, square, window, res, wide, fbuf, st, ds, s0, om, pr, pi, cr, ci, bb, ww, xx, uq, acc, accb, shq, accr, shr, chip,
    xsend, xrecv, zsend, zrecv,
    load_sem, slow_sem, ds_sem, s0_sem, sh_sem, om_sem, acc_sem, shq_sem, x_sem, zs_sem, zr_sem,
):
    points, levels, shots, fronts = dims
    half, quarter = points // 2, points // 4
    total_levels = 2 * levels
    d, f, s = lax.axis_index("depth"), lax.axis_index("freq"), lax.axis_index("shot")
    other_core, other_chip = {"freq": 1 - f}, {"depth": 1 - d}
    provider = f == d

    barrier = pltpu.get_barrier_semaphore()
    pl.semaphore_signal(barrier, inc=1, device_id=other_core, device_id_type=MESH)
    pl.semaphore_signal(barrier, inc=1, device_id=other_chip, device_id_type=MESH)
    for step in range(1, shots):
        pl.semaphore_signal(
            barrier, inc=1, device_id={"shot": lax.rem(s + step, shots)}, device_id_type=MESH
        )

    def load(index, front, field):
        return pltpu.make_async_copy(field.at[0, front], fbuf.at[index], load_sem.at[index])

    def remote(source_ref, target_ref, sems, device, index):
        return pltpu.make_async_remote_copy(
            src_ref=source_ref, dst_ref=target_ref, send_sem=sems.at[0, index],
            recv_sem=sems.at[1, index], device_id=device, device_id_type=MESH,
        )

    def send_field():
        return send_front(source)

    def send_front(field):
        return remote(field.at[0, fronts - 1], fbuf.at[2], sh_sem, other_core, 0)

    def load_slow(j):
        return pltpu.make_async_copy(slowness.at[0, j], slow.at[j], slow_sem.at[j])

    def send_turn():
        return remote(om, om, om_sem, other_core, 0)

    def send_slow(z):
        return remote(ds.at[z], ds.at[z], ds_sem, other_chip, z)

    def send_mean(z):
        return remote(s0.at[z], s0.at[z], s0_sem, other_chip, z)

    def send_image(z):
        return remote(accb.at[z, 1 - f], accr.at[z], acc_sem, other_core, z)

    def send_shared(z):
        return remote(shq.at[z, 1 - f], shr.at[z], shq_sem, other_core, z)

    def send_section(z):
        j = lax.rem(z, levels)
        return remote(xsend.at[j], xrecv.at[j], x_sem, other_chip, j)

    def send_columns(j, step):
        owner = lax.rem(s + step, shots)
        return pltpu.make_async_remote_copy(
            src_ref=zsend.at[j, owner], dst_ref=zrecv.at[j, s], send_sem=zs_sem.at[j, owner],
            recv_sem=zr_sem.at[j, s], device_id={"shot": owner}, device_id_type=MESH,
        )

    def recv_columns(j, step):
        owner = lax.rem(s + step, shots)
        return pltpu.make_async_remote_copy(
            src_ref=zsend.at[j, owner], dst_ref=zrecv.at[j, owner], send_sem=zs_sem.at[j, owner],
            recv_sem=zr_sem.at[j, owner], device_id={"shot": owner}, device_id_type=MESH,
        )

    for j in range(levels):
        load_slow(j).start()
    for front in range(2):
        @pl.when(jnp.logical_and(provider, f == front))
        def _(field=(source, receiver)[front]):
            load(2, fronts - 1, field).start()

    load(0, d, source).start()
    load(1, d, receiver).start()

    def grid_index(axis):
        at = lax.broadcasted_iota(jnp.int32, (points, points), axis)
        odd = jnp.where(at >= half, 1, 0)
        wave = 2 * jnp.where(at - half * odd >= quarter, at - half * odd - quarter, at - half * odd)
        return at, jnp.where(at == quarter, half, wave + odd).astype(F32) * (2.0 * np.pi / points)

    row, row_wave = grid_index(0)
    column, column_wave = grid_index(1)
    square[...] = jnp.square(row_wave) + jnp.square(column_wave)

    table_cos = even_polynomial(np.cos, np.pi**2, 8)
    table_sinc = even_polynomial(sinc, np.pi**2, 8)

    def frequency(axis, part):
        at = lax.broadcasted_iota(jnp.int32, (half, half), axis)
        if part == 1:
            return jnp.where(at < quarter, 2 * at + 1, points - 1 - 2 * (at - quarter))
        mirrored = jnp.where(at == quarter, half, points - 2 * (at - quarter))
        return jnp.where(at < quarter, 2 * at, mirrored)

    for part in range(2):
        for turned in range(2):
            place = lax.broadcasted_iota(jnp.int32, (half, half), turned)
            product = place * frequency(1 - turned, part)
            wrapped = ((product + half) & (points - 1)) - half
            x = wrapped.astype(F32) * (2.0 * np.pi / points)
            cosine = horner(table_cos, x * x).astype(BF16)
            sine = x * horner(table_sinc, x * x)
            upper, lower = ((-sine).astype(BF16), sine.astype(BF16))
            if turned:
                upper, lower = lower, upper
            tab[turned, part, :half, :half] = cosine
            tab[turned, part, half:, half:] = cosine
            tab[turned, part, :half, half:] = upper
            tab[turned, part, half:, :half] = lower

    def taper(at):
        distance_in = (jnp.minimum(at, points - 1 - at) + 1).astype(F32)
        return jnp.minimum(distance_in * (16.0 / points), 1.0)

    window[...] = taper(row) * taper(column) * (1.0 / points)

    pl.semaphore_wait(barrier, shots + 1)
    for front in range(2):
        @pl.when(jnp.logical_and(provider, f == front))
        def _(field=(receiver, source)[front]):
            om[...] = jnp.full((8, points), omegas[0, fronts - 1], F32)
            send_turn().start()
            send_front(field).start()

    for j in range(levels):
        load_slow(j).wait()
        mean = jnp.mean(slow[j])
        ds[d * levels + j] = (slow[j] - mean).astype(BF16)
        s0[d * levels + j] = jnp.full((8, points), mean, F32)
        send_mean(d * levels + j).start()
        send_slow(d * levels + j).start()

    def fold_into(slot, re, im):
        lo, hi = slice(0, half), slice(half, points)
        for at in range(0, points, CHUNK):
            rows, into = slice(at, at + CHUNK), slice(slot * points + at, slot * points + at + CHUNK)
            for lanes, x in ((lo, re), (hi, im)):
                a, b = x[rows, lo], x[rows, hi]
                st[0, into, lanes] = (a + b).astype(BF16)
                st[1, into, lanes] = (a - b).astype(BF16)

    for index, field in enumerate((source, receiver)):
        load(index, d, field).wait()
        fold_into(index, fbuf.at[index, 0], fbuf.at[index, 1])

    @pl.when(provider)
    def _():
        load(2, fronts - 1, source).wait()

    @pl.when(jnp.logical_not(provider))
    def _():
        send_turn().wait_recv()
        send_field().wait_recv()

    fold_into(2, fbuf.at[2, 0], fbuf.at[2, 1])

    turn_own = omegas[0, d]
    sign = (2 * f - 1).astype(F32)
    limit = 1.01 * (FASTEST_TURN * SLOWEST) ** 2
    kz_cos = even_polynomial(np.cos, limit, 5)
    kz_sinc = even_polynomial(sinc, limit, 5)
    limit = 1.01 * (FASTEST_TURN * SLOWNESS_SPAN) ** 2
    turn_cos = even_polynomial(np.cos, limit, 4)
    turn_sinc = even_polynomial(sinc, limit, 3)
    inv = 1.0 / points

    def propagator(index, radius_sq, flip):
        def rows(at, count, targets):
            vertical = radius_sq - square[at : at + count, :]
            size = jnp.abs(vertical)
            root = size * lax.rsqrt(jnp.maximum(size, 1e-30))
            positive = vertical >= 0.0
            x = jnp.maximum(vertical, 0.0)
            re = jnp.where(positive, horner(kz_cos, x), jnp.exp(-root)) * inv
            im = jnp.where(positive, root * horner(kz_sinc, x), 0.0) * (inv * flip)
            for target in targets:
                pr[index, target : target + count, :] = re
                pi[index, target : target + count, :] = im

        step = quarter // 2
        for at in range(0, quarter, step):
            rows(at, step, (at, at + quarter))
            rows(half + at, step, (half + at, half + quarter + at))
        rows(quarter, 8, (quarter,))

    def correction(index, turn, slow):
        step = quarter // 2
        for at in range(0, points, step):
            x = turn * slow[at : at + step, :].astype(F32)
            y = x * x
            w = window[at : at + step, :]
            cr[index, at : at + step, :] = horner(turn_cos, y) * w
            ci[index, at : at + step, :] = horner(turn_sinc, y) * (x * w)

    def dot(a, b):
        return jnp.dot(a, b, preferred_element_type=F32)

    def multiply_right(operand, turned):
        for part in range(2):
            res[part] = dot(operand[part], tab[turned, part])

    def multiply_left(turned, operand):
        for part in range(2):
            wide[part] = dot(tab[turned, part], operand[part])

    def fold_rows():
        for i in range(3):
            for part in range(2):
                lanes = slice(i * points + part * half, i * points + (part + 1) * half)
                for at in range(0, half, CHUNK):
                    row = i * points + at
                    top = res[part, row : row + CHUNK, :]
                    bottom = res[part, half + row : half + row + CHUNK, :]
                    for fold, w in ((0, top + bottom), (1, top - bottom)):
                        bb[fold, at : at + CHUNK, lanes] = w[:, :half].astype(BF16)
                        bb[fold, half + at : half + at + CHUNK, lanes] = w[:, half:].astype(BF16)

    def advance(i, which, sigma):
        lanes = slice(i * points, (i + 1) * points)
        for part in range(2):
            for at in range(0, half, CHUNK):
                rows = slice(part * half + at, part * half + at + CHUNK)
                top, bottom = slice(at, at + CHUNK), slice(half + at, half + at + CHUNK)
                re, im = wide[part, top, lanes], wide[part, bottom, lanes]
                p, q = pr[which, rows, :], pi[which, rows, :]
                if sigma > 0:
                    ww[part, top, lanes] = (re * p - im * q).astype(BF16)
                    ww[part, bottom, lanes] = (re * q + im * p).astype(BF16)
                else:
                    ww[part, top, lanes] = (re * p + im * q).astype(BF16)
                    ww[part, bottom, lanes] = (im * p - re * q).astype(BF16)

    def unfold_rows():
        for i in range(3):
            for at in range(0, points, CHUNK):
                rows, lanes = slice(at, at + CHUNK), slice(i * points, (i + 1) * points)
                even, odd = wide[0, rows, lanes], wide[1, rows, lanes]
                target = i * points + at % half
                lanes = slice(0, half) if at < half else slice(half, points)
                for start_row, y in ((0, even + odd), (half, even - odd)):
                    into = slice(start_row + target, start_row + target + CHUNK)
                    xx[0, into, lanes] = y[:, :half].astype(BF16)
                    xx[1, into, lanes] = y[:, half:].astype(BF16)

    def finish(i, which, sigma, emit):
        for at in range(0, points, CHUNK):
            rows = slice(at, at + CHUNK)
            into = slice(i * points + at, i * points + at + CHUNK)
            even, odd = res[0, into, :], res[1, into, :]
            out = []
            for lanes, y in ((slice(0, half), even + odd), (slice(half, points), even - odd)):
                re, im = y[:, :half], y[:, half:]
                c, t = cr[which, rows, lanes], ci[which, rows, lanes]
                if sigma > 0:
                    out.append((re * c - im * t, re * t + im * c))
                else:
                    out.append((re * c + im * t, im * c - re * t))
            for part in range(2):
                a, b = out[0][part], out[1][part]
                lanes = slice(part * half, (part + 1) * half)
                st[0, into, lanes] = (a + b).astype(BF16)
                st[1, into, lanes] = (a - b).astype(BF16)
            emit(rows, out)

    def combine(z):
        send_image(z).wait_recv()
        send_shared(z).wait_recv()
        total = acc[lax.rem(z, 2), f] + accr[z].astype(F32)
        total += shq[z, f, 0].astype(F32) * shr[z, 0].astype(F32)
        total += shq[z, f, 1].astype(F32) * shr[z, 1].astype(F32)
        mine = lax.div(z, levels) == d

        @pl.when(mine)
        def _():
            chip[lax.rem(z, levels)] = total

        @pl.when(jnp.logical_not(mine))
        def _():
            xsend[lax.rem(z, levels)] = total.astype(BF16)
            send_section(z).start()

    def place(z):
        j = lax.rem(z, levels)
        send_section(z).wait_recv()
        total = (chip[j] + xrecv[j].astype(F32)).astype(BF16)
        columns = lax.broadcasted_iota(jnp.int32, (TILE, points), 0)
        places = lax.broadcasted_iota(jnp.int32, (TILE, points), 1)
        for step in [*range(1, shots), 0]:
            owner = lax.rem(s + step, shots)
            chosen = places == columns + (owner * TILE - start[0])
            chosen = jnp.where(chosen, 1.0, 0.0).astype(BF16)
            zsend[j, owner] = dot(chosen, total).astype(BF16)
            if step > 0:
                send_columns(j, step).start()

    def one_level(z, carry):
        mine = lax.div(z, levels) == d

        @pl.when(jnp.logical_not(mine))
        def _():
            send_mean(z).wait_recv()

        mean = s0[z][0:1, :]
        turn_shared = om[0:1, :]
        multiply_right(st, 0)
        propagator(1, jnp.square(turn_shared * mean), sign)
        propagator(0, jnp.square(turn_own * mean), 1.0)
        fold_rows()
        multiply_left(1, bb)
        advance(2, 1, 1)
        advance(0, 0, -1)
        advance(1, 0, 1)

        @pl.when(jnp.logical_not(mine))
        def _():
            send_slow(z).wait_recv()

        @pl.when(z >= 1)
        def _():
            combine(z - 1)

        def emit_shared(rows, out):
            for side in range(2):
                for part in range(2):
                    shq[z, side, part, rows, :] = out[side][part].astype(BF16)

        def emit_first(rows, out):
            for side in range(2):
                for part in range(2):
                    uq[side, part, rows, :] = out[side][part]

        def emit_second(rows, out):
            for side in range(2):
                product = uq[side, 0, rows, :] * out[side][0] + uq[side, 1, rows, :] * out[side][1]
                acc[lax.rem(z, 2), side, rows, :] = product
                accb[z, side, rows, :] = product.astype(BF16)

        multiply_left(0, ww)
        correction(1, sign * turn_shared, ds.at[z])
        correction(0, turn_own, ds.at[z])
        unfold_rows()
        multiply_right(xx, 1)
        finish(2, 1, 1, emit_shared)
        send_shared(z).start()
        finish(0, 0, -1, emit_first)
        finish(1, 0, 1, emit_second)
        send_image(z).start()

        before = z - 2 + d

        @pl.when(jnp.logical_and(before >= d * levels, before < (d + 1) * levels))
        def _():
            place(before)

        return carry

    lax.fori_loop(0, total_levels, one_level, 0)
    last = total_levels - 1
    combine(last)

    @pl.when(lax.div(last, levels) == d)
    def _():
        place(last)

    for j in range(levels):
        image[0, pl.ds(j, TILE, stride=levels), :] = zsend[j, s].astype(F32)
        total = jnp.zeros((TILE, half), F32)
        for step in range(1, shots):
            recv_columns(j, step).wait_recv()
            total += zrecv[j, lax.rem(s + step, shots)].astype(F32)
        image[1, pl.ds(j, TILE, stride=levels), :] = total

    @pl.when(provider)
    def _():
        send_turn().wait_send()
        send_field().wait_send()

    for j in range(levels):
        send_mean(d * levels + j).wait_send()
        send_slow(d * levels + j).wait_send()
        send_section((1 - d) * levels + j).wait_send()
        for step in range(1, shots):
            send_columns(j, step).wait_send()
    for z in range(total_levels):
        send_image(z).wait_send()
        send_shared(z).wait_send()


def migrate(source, receiver, slowness, omegas, shot_start):
    points = source.shape[-1]
    fronts = source.shape[1]
    levels = slowness.shape[1]
    shots = lax.axis_size("shot")
    total = 2 * levels
    half = points // 2
    full = (points, points)
    side = (points, half)
    vmem, sem = pltpu.VMEM, pltpu.SemaphoreType.DMA
    in_vmem = pl.BlockSpec(memory_space=pltpu.VMEM)
    in_smem = pl.BlockSpec(memory_space=pltpu.SMEM)
    anywhere = pl.BlockSpec(memory_space=pl.ANY)
    terms = pl.pallas_call(
        functools.partial(migrate_kernel, (points, levels, shots, fronts)),
        out_shape=jax.ShapeDtypeStruct((2, TILE * levels, half), F32),
        in_specs=[anywhere, anywhere, anywhere, in_smem, in_smem],
        out_specs=in_vmem,
        scratch_shapes=[
            vmem((2, 2) + full, BF16),
            vmem((levels,) + full, F32),
            vmem(full, F32),
            vmem(full, F32),
            vmem((2, 3 * points, points), F32),
            vmem((2, points, 3 * points), F32),
            vmem((3, 2) + full, F32),
            vmem((2, 3 * points, points), BF16),
            vmem((total,) + full, BF16),
            vmem((total, 8, points), F32),
            vmem((8, points), F32),
            vmem((2,) + full, F32),
            vmem((2,) + full, F32),
            vmem((2,) + full, F32),
            vmem((2,) + full, F32),
            vmem((2, points, 3 * points), BF16),
            vmem((2, points, 3 * points), BF16),
            vmem((2, 3 * points, points), BF16),
            vmem((2, 2) + side, F32),
            vmem((2, 2) + side, F32),
            vmem((total, 2) + side, BF16),
            vmem((total, 2, 2) + side, BF16),
            vmem((total,) + side, BF16),
            vmem((total, 2) + side, BF16),
            vmem((levels,) + side, F32),
            vmem((levels,) + side, BF16),
            vmem((levels,) + side, BF16),
            vmem((levels, shots, TILE, half), BF16),
            vmem((levels, shots, TILE, half), BF16),
            sem((3,)),
            sem((levels,)),
            sem((2, total)),
            sem((2, total)),
            sem((2, 1)),
            sem((2, 1)),
            sem((2, total)),
            sem((2, total)),
            sem((2, levels)),
            sem((levels, shots)),
            sem((levels, shots)),
        ],
        compiler_params=pltpu.CompilerParams(
            collective_id=0, has_side_effects=True, vmem_limit_bytes=60 * 1024 * 1024
        ),
        name="migrate",
    )(source, receiver, slowness, omegas, shot_start)
    return (terms[0] + terms[1]).reshape(TILE, levels, half)


def solution(mesh):
    sizes = mesh.shape

    def per_device(source, receiver, slowness, *rest):
        if sizes["depth"] == 2 and sizes["freq"] == 2 and source.shape[1] == 3 and slowness.shape[1] > 1:
            return migrate(source, receiver, slowness, *rest)
        return local(source, receiver, slowness, *rest)

    return jax.shard_map(
        per_device,
        mesh=mesh,
        in_specs=(
            P(("groups", "shot"), "freq", None, None, None),
            P(("groups", "shot"), "freq", None, None, None),
            P(("groups", "shot"), "depth", None, None),
            P(("groups", "shot"), "freq"),
            P(("groups", "shot")),
        ),
        out_specs=P(("groups", "shot"), "depth", "freq"),
        check_vma=False,
    )
```

```python
import functools

import jax
import jax.numpy as jnp
import numpy as np
from jax import lax
from jax.experimental import pallas as pl
from jax.experimental.pallas import tpu as pltpu
from jax.sharding import PartitionSpec as P

TILE = 128


def from_behind(array, axis, by):
    peers = lax.axis_size(axis)
    pairs = [(i, i + by) for i in range(peers) if 0 <= i + by < peers]
    return lax.ppermute(array, axis, pairs)


def tables(points):
    positions = jnp.arange(points, dtype=jnp.int32)
    product = positions[:, None] * positions[None, :] % points
    angles = 2.0 * jnp.pi / points * product.astype(jnp.float32)
    cosine_table = jnp.cos(angles).astype(jnp.bfloat16)
    sine_table = jnp.sin(angles).astype(jnp.bfloat16)
    forward = jnp.concatenate(
        [
            jnp.concatenate([cosine_table, -sine_table], axis=1),
            jnp.concatenate([sine_table, cosine_table], axis=1),
        ],
        axis=0,
    )
    inverse = jnp.concatenate(
        [
            jnp.concatenate([cosine_table, sine_table], axis=1),
            jnp.concatenate([-sine_table, cosine_table], axis=1),
        ],
        axis=0,
    )
    return (forward, inverse)


def lateral_grids(points):
    positions = jnp.arange(points, dtype=jnp.int32)
    wrapped = (positions + points // 2) % points - points // 2
    wavenumber = 2.0 * jnp.pi / points * wrapped.astype(jnp.float32)
    edge_width = points // 16
    distance_in = jnp.minimum(positions, points - 1 - positions) + 1
    edge_taper = jnp.minimum(distance_in.astype(jnp.float32) / edge_width, 1.0)
    return (wavenumber, edge_taper)


def flip_parts(field_in):
    leading = field_in.shape[:-2]
    row_count = field_in.shape[-2]
    col_count = field_in.shape[-1] // 2
    pieces = field_in.reshape(leading + (row_count, 2, col_count))
    moved = jnp.swapaxes(pieces, -3, -1)
    return moved.reshape(leading + (col_count, 2 * row_count))


def extrapolate(
    wave_state, slow_level, angular, field_signs, forward, inverse, wavenumber, edge_taper
):
    batch_size, points, width = wave_state.shape
    inv_points = 1.0 / points
    half_done = jnp.dot(
        wave_state.reshape(batch_size * points, width), forward, preferred_element_type=jnp.float32
    )
    half_done = flip_parts(half_done.astype(jnp.bfloat16).reshape(batch_size, points, width))
    spectrum = jnp.dot(
        half_done.reshape(batch_size * points, width), forward, preferred_element_type=jnp.float32
    ).reshape(batch_size, points, width)
    mean_slow = jnp.mean(slow_level)
    radius_sq = jnp.square(angular * mean_slow)
    square = jnp.square(wavenumber)[:, None] + jnp.square(wavenumber)[None, :]
    vertical = radius_sq[:, None, None] - square[None]
    real_kz = jnp.sqrt(jnp.maximum(vertical, 0.0))
    damping = jnp.exp(-jnp.sqrt(jnp.maximum(-vertical, 0.0)))
    phase_turn = field_signs[:, None, None] * real_kz
    phase_real = damping * jnp.cos(phase_turn)
    phase_imag = damping * jnp.sin(phase_turn)
    spec_real = spectrum[..., :points]
    spec_imag = spectrum[..., points:]
    shifted = jnp.concatenate(
        [
            spec_real * phase_real - spec_imag * phase_imag,
            spec_real * phase_imag + spec_imag * phase_real,
        ],
        axis=-1,
    ).astype(jnp.bfloat16)
    half_back = (
        jnp.dot(
            shifted.reshape(batch_size * points, width), inverse, preferred_element_type=jnp.float32
        )
        * inv_points
    )
    half_back = flip_parts(half_back.astype(jnp.bfloat16).reshape(batch_size, points, width))
    field_out = (
        jnp.dot(
            half_back.reshape(batch_size * points, width),
            inverse,
            preferred_element_type=jnp.float32,
        ).reshape(batch_size, points, width)
        * inv_points
    )
    correction = (field_signs * angular)[:, None, None] * (slow_level - mean_slow)[None]
    window = edge_taper[:, None] * edge_taper[None, :]
    corr_real = jnp.cos(correction) * window[None]
    corr_imag = jnp.sin(correction) * window[None]
    field_real = field_out[..., :points]
    field_imag = field_out[..., points:]
    return (
        field_real * corr_real - field_imag * corr_imag,
        field_real * corr_imag + field_imag * corr_real,
    )


def local(source, receiver, slowness, omegas, shot_start):
    points = source.shape[-1]
    fronts = source.shape[1]
    levels = slowness.shape[1]
    segments = lax.axis_size("depth")
    segment_index = lax.axis_index("depth")
    forward, inverse = tables(points)
    wavenumber, edge_taper = lateral_grids(points)
    field_signs = jnp.array([-1.0, 1.0], jnp.float32)

    def surface(chosen):
        src_front = lax.dynamic_index_in_dim(source[0], chosen, 0, keepdims=False)
        rcv_front = lax.dynamic_index_in_dim(receiver[0], chosen, 0, keepdims=False)
        paired = jnp.stack([src_front, rcv_front])
        return jnp.concatenate([paired[:, 0], paired[:, 1]], axis=-1).astype(jnp.bfloat16)

    def extrapolate_front(operands):
        wave_state, rate_now = operands
        angular = jnp.stack([rate_now, rate_now])
        level_terms = []
        for level_index in range(levels):
            real_part, imag_part = extrapolate(
                wave_state,
                slowness[0, level_index],
                angular,
                field_signs,
                forward,
                inverse,
                wavenumber,
                edge_taper,
            )
            level_terms.append(real_part[0] * real_part[1] + imag_part[0] * imag_part[1])
            wave_state = jnp.concatenate([real_part, imag_part], axis=-1).astype(jnp.bfloat16)
        return (wave_state, jnp.stack(level_terms, axis=1))

    def stay_still(operands):
        wave_state, rate_now = operands
        return (jnp.zeros_like(wave_state), jnp.zeros((points, levels, points), jnp.float32))

    def one_turn(turn_index, carry):
        incoming, image_sum = carry
        front_index = turn_index - segment_index
        active = jnp.logical_and(front_index >= 0, front_index < fronts)
        chosen = jnp.clip(front_index, 0, fronts - 1)
        begin_field = jnp.where(segment_index == 0, surface(chosen), incoming)
        rate_now = lax.dynamic_index_in_dim(omegas[0], chosen, 0, keepdims=False)
        wave_state, level_image = lax.cond(
            active, extrapolate_front, stay_still, (begin_field, rate_now)
        )
        incoming = from_behind(wave_state, "depth", 1)
        return (incoming, image_sum + level_image)

    initial = (
        jnp.zeros((2, points, 2 * points), jnp.bfloat16),
        jnp.zeros((points, levels, points), jnp.float32),
    )
    final_carry = lax.fori_loop(0, segments + fronts - 1, one_turn, initial)
    local_image = lax.psum_scatter(
        final_carry[1].astype(jnp.bfloat16), "freq", scatter_dimension=2, tiled=True
    ).astype(jnp.float32)
    aperture_start = shot_start[0]
    owners = lax.axis_size("shot")
    survey_cols = owners * TILE
    padding = jnp.zeros((survey_cols,) + local_image.shape[1:], jnp.float32)
    padded = jnp.concatenate([padding, local_image, padding], axis=0)
    offset = jnp.clip(
        jnp.zeros((), jnp.int32) - aperture_start + survey_cols, 0, points + survey_cols
    )
    placed = lax.dynamic_slice_in_dim(padded, offset, survey_cols, 0)
    blocks = placed.reshape((owners, TILE) + local_image.shape[1:])
    received = lax.all_to_all(
        blocks.astype(jnp.bfloat16), "shot", split_axis=0, concat_axis=0, tiled=True
    ).astype(blocks.dtype)
    collected = jnp.sum(received, axis=0)
    return collected


MESH = pl.DeviceIdType.MESH
BF16 = jnp.bfloat16
CHUNK = 32
LOG2_E = 1.4426950408889634
F32 = jnp.float32
SLOWEST, SLOWNESS_SPAN, FASTEST_TURN = 1.4, 0.8, 2.5


def even_polynomial(function, limit, degree):
    series = np.polynomial.chebyshev.Chebyshev.interpolate(
        lambda x: function(np.sqrt(np.maximum(x, 0.0))), degree, domain=[0.0, limit]
    )
    return [float(c) for c in series.convert(kind=np.polynomial.Polynomial).coef]


def horner(coefficients, x):
    total = coefficients[-1] * x + coefficients[-2]
    for c in coefficients[-3::-1]:
        total = total * x + c
    return total


def sinc(y):
    return np.sinc(y / np.pi)


def migrate_kernel(
    dims, source, receiver, slowness, omegas, start, image,
    tab, slow, square, window, res, fbuf, st, ds, s0, om, pr, pi, cr, ci, bb, ww, xx, uq, acc, accb, shq, accr, shr, chip,
    xsend, xrecv, zsend, zrecv,
    load_sem, slow_sem, ds_sem, s0_sem, sh_sem, om_sem, acc_sem, shq_sem, x_sem, zs_sem, zr_sem,
):
    points, levels, shots, fronts = dims
    half, quarter = points // 2, points // 4
    total_levels = 2 * levels
    d, f, s = lax.axis_index("depth"), lax.axis_index("freq"), lax.axis_index("shot")
    other_core, other_chip = {"freq": 1 - f}, {"depth": 1 - d}
    provider = f == d

    barrier = pltpu.get_barrier_semaphore()
    pl.semaphore_signal(barrier, inc=1, device_id=other_core, device_id_type=MESH)
    pl.semaphore_signal(barrier, inc=1, device_id=other_chip, device_id_type=MESH)
    for step in range(1, shots):
        pl.semaphore_signal(
            barrier, inc=1, device_id={"shot": lax.rem(s + step, shots)}, device_id_type=MESH
        )

    def load(index, front, field):
        return pltpu.make_async_copy(field.at[0, front], fbuf.at[index], load_sem.at[index])

    def remote(source_ref, target_ref, sems, device, index):
        return pltpu.make_async_remote_copy(
            src_ref=source_ref, dst_ref=target_ref, send_sem=sems.at[0, index],
            recv_sem=sems.at[1, index], device_id=device, device_id_type=MESH,
        )

    def send_field():
        return send_front(source)

    def send_front(field):
        return remote(field.at[0, fronts - 1], fbuf.at[2], sh_sem, other_core, 0)

    def load_slow(j):
        return pltpu.make_async_copy(slowness.at[0, j], slow.at[j], slow_sem.at[j])

    def send_turn():
        return remote(om, om, om_sem, other_core, 0)

    def send_slow(z):
        return remote(ds.at[z], ds.at[z], ds_sem, other_chip, z)

    def send_mean(z):
        return remote(s0.at[z], s0.at[z], s0_sem, other_chip, z)

    def send_image(z):
        return remote(accb.at[z, 1 - f], accr.at[z], acc_sem, other_core, z)

    def send_shared(z):
        return remote(shq.at[z, 1 - f], shr.at[z], shq_sem, other_core, z)

    def send_section(z):
        j = lax.rem(z, levels)
        return remote(xsend.at[j], xrecv.at[j], x_sem, other_chip, j)

    def send_columns(j, step):
        owner = lax.rem(s + step, shots)
        return pltpu.make_async_remote_copy(
            src_ref=zsend.at[j, owner], dst_ref=zrecv.at[j, s], send_sem=zs_sem.at[j, owner],
            recv_sem=zr_sem.at[j, s], device_id={"shot": owner}, device_id_type=MESH,
        )

    def recv_columns(j, step):
        owner = lax.rem(s + step, shots)
        return pltpu.make_async_remote_copy(
            src_ref=zsend.at[j, owner], dst_ref=zrecv.at[j, owner], send_sem=zs_sem.at[j, owner],
            recv_sem=zr_sem.at[j, owner], device_id={"shot": owner}, device_id_type=MESH,
        )

    for j in range(levels):
        load_slow(j).start()
    for front in range(2):
        @pl.when(jnp.logical_and(provider, f == front))
        def _(field=(source, receiver)[front]):
            load(2, fronts - 1, field).start()

    load(0, d, source).start()
    load(1, d, receiver).start()

    def grid_index(axis):
        at = lax.broadcasted_iota(jnp.int32, (points, points), axis)
        odd = jnp.where(at >= half, 1, 0)
        wave = 2 * jnp.where(at - half * odd >= quarter, at - half * odd - quarter, at - half * odd)
        return at, jnp.where(at == quarter, half, wave + odd).astype(F32) * (2.0 * np.pi / points)

    row, row_wave = grid_index(0)
    column, column_wave = grid_index(1)
    square[...] = jnp.square(row_wave) + jnp.square(column_wave)

    table_cos = even_polynomial(np.cos, np.pi**2, 8)
    table_sinc = even_polynomial(sinc, np.pi**2, 8)

    def frequency(axis, part):
        at = lax.broadcasted_iota(jnp.int32, (half, half), axis)
        if part == 1:
            return jnp.where(at < quarter, 2 * at + 1, points - 1 - 2 * (at - quarter))
        mirrored = jnp.where(at == quarter, half, points - 2 * (at - quarter))
        return jnp.where(at < quarter, 2 * at, mirrored)

    for part in range(2):
        for turned in range(2):
            place = lax.broadcasted_iota(jnp.int32, (half, half), turned)
            product = place * frequency(1 - turned, part)
            wrapped = ((product + half) & (points - 1)) - half
            x = wrapped.astype(F32) * (2.0 * np.pi / points)
            cosine = horner(table_cos, x * x).astype(BF16)
            sine = x * horner(table_sinc, x * x)
            upper, lower = ((-sine).astype(BF16), sine.astype(BF16))
            if turned:
                upper, lower = lower, upper
            tab[turned, part, :half, :half] = cosine
            tab[turned, part, half:, half:] = cosine
            tab[turned, part, :half, half:] = upper
            tab[turned, part, half:, :half] = lower

    def taper(at):
        distance_in = (jnp.minimum(at, points - 1 - at) + 1).astype(F32)
        return jnp.minimum(distance_in * (16.0 / points), 1.0)

    window[...] = taper(row) * taper(column) * (1.0 / points**2)

    pl.semaphore_wait(barrier, shots + 1)
    for front in range(2):
        @pl.when(jnp.logical_and(provider, f == front))
        def _(field=(receiver, source)[front]):
            om[...] = jnp.full((8, points), omegas[fronts - 1], F32)
            send_turn().start()
            send_front(field).start()

    for j in range(levels):
        load_slow(j).wait()
        mean = jnp.mean(slow[j])
        ds[d * levels + j] = (slow[j] - mean).astype(BF16)
        s0[d * levels + j] = jnp.full((8, points), mean, F32)
        send_mean(d * levels + j).start()
        send_slow(d * levels + j).start()

    def fold_into(slot, re, im):
        lo, hi = slice(0, half), slice(half, points)
        for at in range(0, points, CHUNK):
            rows, into = slice(at, at + CHUNK), slice(slot * points + at, slot * points + at + CHUNK)
            for lanes, x in ((lo, re), (hi, im)):
                a, b = x[rows, lo], x[rows, hi]
                st[0, into, lanes] = (a + b).astype(BF16)
                st[1, into, lanes] = (a - b).astype(BF16)

    for index, field in enumerate((source, receiver)):
        load(index, d, field).wait()
        fold_into(index, fbuf.at[index, 0], fbuf.at[index, 1])

    @pl.when(provider)
    def _():
        load(2, fronts - 1, source).wait()

    @pl.when(jnp.logical_not(provider))
    def _():
        send_turn().wait_recv()
        send_field().wait_recv()

    fold_into(2, fbuf.at[2, 0], fbuf.at[2, 1])

    turn_own = omegas[d]
    sign = (2 * f - 1).astype(F32)
    limit = 1.01 * (FASTEST_TURN * SLOWEST) ** 2
    kz_cos = even_polynomial(np.cos, limit, 5)
    kz_sinc = even_polynomial(sinc, limit, 5)
    limit = 1.01 * (FASTEST_TURN * SLOWNESS_SPAN) ** 2
    turn_cos = even_polynomial(np.cos, limit, 4)
    turn_sinc = even_polynomial(sinc, limit, 3)

    def propagator(index, radius_sq, flip):
        def rows(at, count, targets):
            vertical = radius_sq - square[at : at + count, :]
            size = jnp.abs(vertical)
            root = size * lax.rsqrt(jnp.maximum(size, 1e-30))
            positive = vertical >= 0.0
            x = jnp.maximum(vertical, 0.0)
            re = jnp.where(positive, horner(kz_cos, x), jnp.exp2(root * -LOG2_E))
            im = jnp.where(positive, root * horner(kz_sinc, x), 0.0)
            im = im if flip is None else im * flip
            for target in targets:
                pr[index, target : target + count, :] = re
                pi[index, target : target + count, :] = im

        step = quarter // 2
        for at in range(0, quarter, step):
            rows(at, step, (at, at + quarter))
            rows(half + at, step, (half + at, half + quarter + at))
        rows(quarter, 8, (quarter,))

    def correction(index, turn, slow):
        step = quarter // 2
        for at in range(0, points, step):
            x = turn * slow[at : at + step, :].astype(F32)
            y = x * x
            w = window[at : at + step, :]
            cr[index, at : at + step, :] = horner(turn_cos, y) * w
            ci[index, at : at + step, :] = horner(turn_sinc, y) * (x * w)

    def dot(a, b):
        return jnp.dot(a, b, preferred_element_type=F32)

    def transform_all():
        for part in range(2):
            res[part] = dot(st[part], tab[0, part])
        for i in range(3):
            for part in range(2):
                lanes = slice(part * half, (part + 1) * half)
                for at in range(0, half, CHUNK):
                    row = i * points + at
                    top = res[part, row : row + CHUNK, :]
                    bottom = res[part, half + row : half + row + CHUNK, :]
                    for fold, w in ((0, top + bottom), (1, top - bottom)):
                        bb[i, fold, at : at + CHUNK, lanes] = w[:, :half].astype(BF16)
                        bb[i, fold, half + at : half + at + CHUNK, lanes] = w[:, half:].astype(BF16)

    def advance(i, which, sigma):
        for part in range(2):
            base = i * points
            res[part, base : base + points, :] = dot(tab[1, part], bb[i, part])
            for at in range(0, half, CHUNK):
                rows = slice(part * half + at, part * half + at + CHUNK)
                top, bottom = slice(at, at + CHUNK), slice(half + at, half + at + CHUNK)
                re = res[part, base + at : base + at + CHUNK, :]
                im = res[part, base + half + at : base + half + at + CHUNK, :]
                p, q = pr[which, rows, :], pi[which, rows, :]
                if sigma > 0:
                    ww[i, part, top, :] = (re * p - im * q).astype(BF16)
                    ww[i, part, bottom, :] = (re * q + im * p).astype(BF16)
                else:
                    ww[i, part, top, :] = (re * p + im * q).astype(BF16)
                    ww[i, part, bottom, :] = (im * p - re * q).astype(BF16)

    def back(i):
        for part in range(2):
            res[part, i * points : (i + 1) * points, :] = dot(tab[0, part], ww[i, part])
        for at in range(0, points, CHUNK):
            rows = slice(i * points + at, i * points + at + CHUNK)
            even, odd = res[0, rows, :], res[1, rows, :]
            target = at % half
            lanes = slice(0, half) if at < half else slice(half, points)
            for start_row, y in ((0, even + odd), (half, even - odd)):
                into = slice(start_row + target, start_row + target + CHUNK)
                xx[i, 0, into, lanes] = y[:, :half].astype(BF16)
                xx[i, 1, into, lanes] = y[:, half:].astype(BF16)

    def finish(i, which, sigma, emit):
        for part in range(2):
            res[part, i * points : (i + 1) * points, :] = dot(xx[i, part], tab[1, part])
        for at in range(0, points, CHUNK):
            rows = slice(at, at + CHUNK)
            into = slice(i * points + at, i * points + at + CHUNK)
            even, odd = res[0, into, :], res[1, into, :]
            out = []
            for lanes, y in ((slice(0, half), even + odd), (slice(half, points), even - odd)):
                re, im = y[:, :half], y[:, half:]
                c, t = cr[which, rows, lanes], ci[which, rows, lanes]
                if sigma > 0:
                    out.append((re * c - im * t, re * t + im * c))
                else:
                    out.append((re * c + im * t, im * c - re * t))
            for part in range(2):
                a, b = out[0][part], out[1][part]
                lanes = slice(part * half, (part + 1) * half)
                st[0, into, lanes] = (a + b).astype(BF16)
                st[1, into, lanes] = (a - b).astype(BF16)
            emit(rows, out)

    def combine(z):
        send_image(z).wait_recv()
        send_shared(z).wait_recv()
        total = acc[lax.rem(z, 2), f] + accr[z].astype(F32)
        total += shq[z, f, 0].astype(F32) * shr[z, 0].astype(F32)
        total += shq[z, f, 1].astype(F32) * shr[z, 1].astype(F32)
        mine = lax.div(z, levels) == d

        @pl.when(mine)
        def _():
            chip[lax.rem(z, levels)] = total

        @pl.when(jnp.logical_not(mine))
        def _():
            xsend[lax.rem(z, levels)] = total.astype(BF16)
            send_section(z).start()

    def place(z):
        j = lax.rem(z, levels)
        send_section(z).wait_recv()
        total = (chip[j] + xrecv[j].astype(F32)).astype(BF16)
        columns = lax.broadcasted_iota(jnp.int32, (TILE, points), 0)
        places = lax.broadcasted_iota(jnp.int32, (TILE, points), 1)
        for step in [*range(1, shots), 0]:
            owner = lax.rem(s + step, shots)
            chosen = places == columns + (owner * TILE - start[0])
            chosen = jnp.where(chosen, 1.0, 0.0).astype(BF16)
            zsend[j, owner] = dot(chosen, total).astype(BF16)
            if step > 0:
                send_columns(j, step).start()

    def one_level(z, carry):
        mine = lax.div(z, levels) == d

        @pl.when(jnp.logical_not(mine))
        def _():
            send_mean(z).wait_recv()

        mean = s0[z][0:1, :]
        turn_shared = om[0:1, :]
        transform_all()
        propagator(1, jnp.square(turn_shared * mean), sign)
        propagator(0, jnp.square(turn_own * mean), None)
        advance(2, 1, 1)
        back(2)
        advance(0, 0, -1)
        advance(1, 0, 1)

        @pl.when(jnp.logical_not(mine))
        def _():
            send_slow(z).wait_recv()

        @pl.when(z >= 1)
        def _():
            combine(z - 1)

        def emit_shared(rows, out):
            for side in range(2):
                for part in range(2):
                    shq[z, side, part, rows, :] = out[side][part].astype(BF16)

        def emit_first(rows, out):
            for side in range(2):
                for part in range(2):
                    uq[side, part, rows, :] = out[side][part]

        def emit_second(rows, out):
            for side in range(2):
                product = uq[side, 0, rows, :] * out[side][0] + uq[side, 1, rows, :] * out[side][1]
                acc[lax.rem(z, 2), side, rows, :] = product
                accb[z, side, rows, :] = product.astype(BF16)

        correction(1, sign * turn_shared, ds.at[z])
        finish(2, 1, 1, emit_shared)
        send_shared(z).start()
        correction(0, turn_own, ds.at[z])
        back(0)
        back(1)
        before = z - 2 + d

        @pl.when(jnp.logical_and(before >= d * levels, before < (d + 1) * levels))
        def _():
            place(before)

        finish(0, 0, -1, emit_first)
        finish(1, 0, 1, emit_second)
        send_image(z).start()

        return carry

    lax.fori_loop(0, total_levels, one_level, 0)
    last = total_levels - 1
    combine(last)

    @pl.when(lax.div(last, levels) == d)
    def _():
        place(last)

    for j in range(levels):
        total = zsend[j, s].astype(F32)
        for step in range(1, shots):
            recv_columns(j, step).wait_recv()
            total += zrecv[j, lax.rem(s + step, shots)].astype(F32)
        image[pl.ds(j, TILE, stride=levels), :] = total

    @pl.when(provider)
    def _():
        send_turn().wait_send()
        send_field().wait_send()

    for j in range(levels):
        send_mean(d * levels + j).wait_send()
        send_slow(d * levels + j).wait_send()
        send_section((1 - d) * levels + j).wait_send()
        for step in range(1, shots):
            send_columns(j, step).wait_send()
    for z in range(total_levels):
        send_image(z).wait_send()
        send_shared(z).wait_send()


def migrate(source, receiver, slowness, omegas, shot_start):
    points = source.shape[-1]
    fronts = source.shape[1]
    levels = slowness.shape[1]
    shots = lax.axis_size("shot")
    total = 2 * levels
    half = points // 2
    full = (points, points)
    side = (points, half)
    vmem, sem = pltpu.VMEM, pltpu.SemaphoreType.DMA
    in_vmem = pl.BlockSpec(memory_space=pltpu.VMEM)
    in_smem = pl.BlockSpec(memory_space=pltpu.SMEM)
    anywhere = pl.BlockSpec(memory_space=pltpu.HBM)
    return pl.pallas_call(
        functools.partial(migrate_kernel, (points, levels, shots, fronts)),
        out_shape=jax.ShapeDtypeStruct((TILE * levels, half), F32),
        in_specs=[anywhere, anywhere, anywhere, in_smem, in_smem],
        out_specs=in_vmem,
        scratch_shapes=[
            vmem((2, 2) + full, BF16),
            vmem((levels,) + full, F32),
            vmem(full, F32),
            vmem(full, F32),
            vmem((2, 3 * points, points), F32),
            vmem((3, 2) + full, F32),
            vmem((2, 3 * points, points), BF16),
            vmem((total,) + full, BF16),
            vmem((total, 8, points), F32),
            vmem((8, points), F32),
            vmem((2,) + full, F32),
            vmem((2,) + full, F32),
            vmem((2,) + full, F32),
            vmem((2,) + full, F32),
            vmem((3, 2) + full, BF16),
            vmem((3, 2) + full, BF16),
            vmem((3, 2) + full, BF16),
            vmem((2, 2) + side, F32),
            vmem((2, 2) + side, F32),
            vmem((total, 2) + side, BF16),
            vmem((total, 2, 2) + side, BF16),
            vmem((total,) + side, BF16),
            vmem((total, 2) + side, BF16),
            vmem((levels,) + side, F32),
            vmem((levels,) + side, BF16),
            vmem((levels,) + side, BF16),
            vmem((levels, shots, TILE, half), BF16),
            vmem((levels, shots, TILE, half), BF16),
            sem((3,)),
            sem((levels,)),
            sem((2, total)),
            sem((2, total)),
            sem((2, 1)),
            sem((2, 1)),
            sem((2, total)),
            sem((2, total)),
            sem((2, levels)),
            sem((levels, shots)),
            sem((levels, shots)),
        ],
        compiler_params=pltpu.CompilerParams(
            collective_id=0, has_side_effects=True, vmem_limit_bytes=55000 * 1024
        ),
        name="migrate",
    )(source, receiver, slowness, omegas.reshape(-1), shot_start).reshape(TILE, levels, half)


def solution(mesh):
    sizes = mesh.shape

    def per_device(source, receiver, slowness, *rest):
        if sizes["depth"] == 2 and sizes["freq"] == 2 and source.shape[1] == 3 and slowness.shape[1] > 1:
            return migrate(source, receiver, slowness, *rest)
        return local(source, receiver, slowness, *rest)

    return jax.shard_map(
        per_device,
        mesh=mesh,
        in_specs=(
            P(("groups", "shot"), "freq", None, None, None),
            P(("groups", "shot"), "freq", None, None, None),
            P(("groups", "shot"), "depth", None, None),
            P(("groups", "shot"), "freq"),
            P(("groups", "shot")),
        ),
        out_specs=P(("groups", "shot"), "depth", "freq"),
        check_vma=False,
    )
```

```python
import functools

import jax
import jax.numpy as jnp
import numpy as np
from jax import lax
from jax.experimental import pallas as pl
from jax.experimental.pallas import tpu as pltpu
from jax.sharding import PartitionSpec as P

TILE = 128


def from_behind(array, axis, by):
    peers = lax.axis_size(axis)
    pairs = [(i, i + by) for i in range(peers) if 0 <= i + by < peers]
    return lax.ppermute(array, axis, pairs)


def tables(points):
    positions = jnp.arange(points, dtype=jnp.int32)
    product = positions[:, None] * positions[None, :] % points
    angles = 2.0 * jnp.pi / points * product.astype(jnp.float32)
    cosine_table = jnp.cos(angles).astype(jnp.bfloat16)
    sine_table = jnp.sin(angles).astype(jnp.bfloat16)
    forward = jnp.concatenate(
        [
            jnp.concatenate([cosine_table, -sine_table], axis=1),
            jnp.concatenate([sine_table, cosine_table], axis=1),
        ],
        axis=0,
    )
    inverse = jnp.concatenate(
        [
            jnp.concatenate([cosine_table, sine_table], axis=1),
            jnp.concatenate([-sine_table, cosine_table], axis=1),
        ],
        axis=0,
    )
    return (forward, inverse)


def lateral_grids(points):
    positions = jnp.arange(points, dtype=jnp.int32)
    wrapped = (positions + points // 2) % points - points // 2
    wavenumber = 2.0 * jnp.pi / points * wrapped.astype(jnp.float32)
    edge_width = points // 16
    distance_in = jnp.minimum(positions, points - 1 - positions) + 1
    edge_taper = jnp.minimum(distance_in.astype(jnp.float32) / edge_width, 1.0)
    return (wavenumber, edge_taper)


def flip_parts(field_in):
    leading = field_in.shape[:-2]
    row_count = field_in.shape[-2]
    col_count = field_in.shape[-1] // 2
    pieces = field_in.reshape(leading + (row_count, 2, col_count))
    moved = jnp.swapaxes(pieces, -3, -1)
    return moved.reshape(leading + (col_count, 2 * row_count))


def extrapolate(
    wave_state, slow_level, angular, field_signs, forward, inverse, wavenumber, edge_taper
):
    batch_size, points, width = wave_state.shape
    inv_points = 1.0 / points
    half_done = jnp.dot(
        wave_state.reshape(batch_size * points, width), forward, preferred_element_type=jnp.float32
    )
    half_done = flip_parts(half_done.astype(jnp.bfloat16).reshape(batch_size, points, width))
    spectrum = jnp.dot(
        half_done.reshape(batch_size * points, width), forward, preferred_element_type=jnp.float32
    ).reshape(batch_size, points, width)
    mean_slow = jnp.mean(slow_level)
    radius_sq = jnp.square(angular * mean_slow)
    square = jnp.square(wavenumber)[:, None] + jnp.square(wavenumber)[None, :]
    vertical = radius_sq[:, None, None] - square[None]
    real_kz = jnp.sqrt(jnp.maximum(vertical, 0.0))
    damping = jnp.exp(-jnp.sqrt(jnp.maximum(-vertical, 0.0)))
    phase_turn = field_signs[:, None, None] * real_kz
    phase_real = damping * jnp.cos(phase_turn)
    phase_imag = damping * jnp.sin(phase_turn)
    spec_real = spectrum[..., :points]
    spec_imag = spectrum[..., points:]
    shifted = jnp.concatenate(
        [
            spec_real * phase_real - spec_imag * phase_imag,
            spec_real * phase_imag + spec_imag * phase_real,
        ],
        axis=-1,
    ).astype(jnp.bfloat16)
    half_back = (
        jnp.dot(
            shifted.reshape(batch_size * points, width), inverse, preferred_element_type=jnp.float32
        )
        * inv_points
    )
    half_back = flip_parts(half_back.astype(jnp.bfloat16).reshape(batch_size, points, width))
    field_out = (
        jnp.dot(
            half_back.reshape(batch_size * points, width),
            inverse,
            preferred_element_type=jnp.float32,
        ).reshape(batch_size, points, width)
        * inv_points
    )
    correction = (field_signs * angular)[:, None, None] * (slow_level - mean_slow)[None]
    window = edge_taper[:, None] * edge_taper[None, :]
    corr_real = jnp.cos(correction) * window[None]
    corr_imag = jnp.sin(correction) * window[None]
    field_real = field_out[..., :points]
    field_imag = field_out[..., points:]
    return (
        field_real * corr_real - field_imag * corr_imag,
        field_real * corr_imag + field_imag * corr_real,
    )


def local(source, receiver, slowness, omegas, shot_start):
    points = source.shape[-1]
    fronts = source.shape[1]
    levels = slowness.shape[1]
    segments = lax.axis_size("depth")
    segment_index = lax.axis_index("depth")
    forward, inverse = tables(points)
    wavenumber, edge_taper = lateral_grids(points)
    field_signs = jnp.array([-1.0, 1.0], jnp.float32)

    def surface(chosen):
        src_front = lax.dynamic_index_in_dim(source[0], chosen, 0, keepdims=False)
        rcv_front = lax.dynamic_index_in_dim(receiver[0], chosen, 0, keepdims=False)
        paired = jnp.stack([src_front, rcv_front])
        return jnp.concatenate([paired[:, 0], paired[:, 1]], axis=-1).astype(jnp.bfloat16)

    def extrapolate_front(operands):
        wave_state, rate_now = operands
        angular = jnp.stack([rate_now, rate_now])
        level_terms = []
        for level_index in range(levels):
            real_part, imag_part = extrapolate(
                wave_state,
                slowness[0, level_index],
                angular,
                field_signs,
                forward,
                inverse,
                wavenumber,
                edge_taper,
            )
            level_terms.append(real_part[0] * real_part[1] + imag_part[0] * imag_part[1])
            wave_state = jnp.concatenate([real_part, imag_part], axis=-1).astype(jnp.bfloat16)
        return (wave_state, jnp.stack(level_terms, axis=1))

    def stay_still(operands):
        wave_state, rate_now = operands
        return (jnp.zeros_like(wave_state), jnp.zeros((points, levels, points), jnp.float32))

    def one_turn(turn_index, carry):
        incoming, image_sum = carry
        front_index = turn_index - segment_index
        active = jnp.logical_and(front_index >= 0, front_index < fronts)
        chosen = jnp.clip(front_index, 0, fronts - 1)
        begin_field = jnp.where(segment_index == 0, surface(chosen), incoming)
        rate_now = lax.dynamic_index_in_dim(omegas[0], chosen, 0, keepdims=False)
        wave_state, level_image = lax.cond(
            active, extrapolate_front, stay_still, (begin_field, rate_now)
        )
        incoming = from_behind(wave_state, "depth", 1)
        return (incoming, image_sum + level_image)

    initial = (
        jnp.zeros((2, points, 2 * points), jnp.bfloat16),
        jnp.zeros((points, levels, points), jnp.float32),
    )
    final_carry = lax.fori_loop(0, segments + fronts - 1, one_turn, initial)
    local_image = lax.psum_scatter(
        final_carry[1].astype(jnp.bfloat16), "freq", scatter_dimension=2, tiled=True
    ).astype(jnp.float32)
    aperture_start = shot_start[0]
    owners = lax.axis_size("shot")
    survey_cols = owners * TILE
    padding = jnp.zeros((survey_cols,) + local_image.shape[1:], jnp.float32)
    padded = jnp.concatenate([padding, local_image, padding], axis=0)
    offset = jnp.clip(
        jnp.zeros((), jnp.int32) - aperture_start + survey_cols, 0, points + survey_cols
    )
    placed = lax.dynamic_slice_in_dim(padded, offset, survey_cols, 0)
    blocks = placed.reshape((owners, TILE) + local_image.shape[1:])
    received = lax.all_to_all(
        blocks.astype(jnp.bfloat16), "shot", split_axis=0, concat_axis=0, tiled=True
    ).astype(blocks.dtype)
    collected = jnp.sum(received, axis=0)
    return collected


MESH = pl.DeviceIdType.MESH
BF16 = jnp.bfloat16
CHUNK = 32
LOG2_E = 1.4426950408889634
F32 = jnp.float32
SLOWEST, SLOWNESS_SPAN, FASTEST_TURN = 1.4, 0.8, 2.5


def even_polynomial(function, limit, degree):
    series = np.polynomial.chebyshev.Chebyshev.interpolate(
        lambda x: function(np.sqrt(np.maximum(x, 0.0))), degree, domain=[0.0, limit]
    )
    return [float(c) for c in series.convert(kind=np.polynomial.Polynomial).coef]


def horner(coefficients, x):
    total = coefficients[-1] * x + coefficients[-2]
    for c in coefficients[-3::-1]:
        total = total * x + c
    return total


def sinc(y):
    return np.sinc(y / np.pi)


def migrate_kernel(
    dims, source, receiver, slowness, omegas, start, image,
    tab, slow, square, window, res, fbuf, st, ds, s0, om, pr, pi, cr, ci, bb, ww, xx, uq, acc, accb, shq, accr, shr, chip,
    xsend, xrecv, zsend, zrecv,
    load_sem, slow_sem, ds_sem, s0_sem, sh_sem, om_sem, acc_sem, shq_sem, x_sem, zs_sem, zr_sem,
):
    points, levels, shots, fronts = dims
    half, quarter = points // 2, points // 4
    total_levels = 2 * levels
    d, f, s = lax.axis_index("depth"), lax.axis_index("freq"), lax.axis_index("shot")
    other_core, other_chip = {"freq": 1 - f}, {"depth": 1 - d}
    provider = f == d

    barrier = pltpu.get_barrier_semaphore()
    pl.semaphore_signal(barrier, inc=1, device_id=other_core, device_id_type=MESH)
    pl.semaphore_signal(barrier, inc=1, device_id=other_chip, device_id_type=MESH)
    for step in range(1, shots):
        pl.semaphore_signal(
            barrier, inc=1, device_id={"shot": lax.rem(s + step, shots)}, device_id_type=MESH
        )

    def load(index, front, field):
        return pltpu.make_async_copy(field.at[0, front], fbuf.at[index], load_sem.at[index])

    def remote(source_ref, target_ref, sems, device, index):
        return pltpu.make_async_remote_copy(
            src_ref=source_ref, dst_ref=target_ref, send_sem=sems.at[0, index],
            recv_sem=sems.at[1, index], device_id=device, device_id_type=MESH,
        )

    def send_field():
        return send_front(source)

    def send_front(field):
        return remote(field.at[0, fronts - 1], fbuf.at[2], sh_sem, other_core, 0)

    def load_slow(j):
        return pltpu.make_async_copy(slowness.at[0, j], slow.at[j], slow_sem.at[j])

    def send_turn():
        return remote(om, om, om_sem, other_core, 0)

    def send_slow(z):
        return remote(ds.at[z], ds.at[z], ds_sem, other_chip, z)

    def send_mean(z):
        return remote(s0.at[z], s0.at[z], s0_sem, other_chip, z)

    def send_image(z):
        return remote(accb.at[z, 1 - f], accr.at[z], acc_sem, other_core, z)

    def send_shared(z):
        return remote(shq.at[z, 1 - f], shr.at[z], shq_sem, other_core, z)

    def send_section(z):
        j = lax.rem(z, levels)
        return remote(xsend.at[j], xrecv.at[j], x_sem, other_chip, j)

    def send_columns(j, step):
        owner = lax.rem(s + step, shots)
        return pltpu.make_async_remote_copy(
            src_ref=zsend.at[j, owner], dst_ref=zrecv.at[j, s], send_sem=zs_sem.at[j, owner],
            recv_sem=zr_sem.at[j, s], device_id={"shot": owner}, device_id_type=MESH,
        )

    def recv_columns(j, step):
        owner = lax.rem(s + step, shots)
        return pltpu.make_async_remote_copy(
            src_ref=zsend.at[j, owner], dst_ref=zrecv.at[j, owner], send_sem=zs_sem.at[j, owner],
            recv_sem=zr_sem.at[j, owner], device_id={"shot": owner}, device_id_type=MESH,
        )

    for j in range(levels):
        load_slow(j).start()
    for front in range(2):
        @pl.when(jnp.logical_and(provider, f == front))
        def _(field=(source, receiver)[front]):
            load(2, fronts - 1, field).start()

    load(0, d, source).start()
    load(1, d, receiver).start()

    def grid_index(axis):
        at = lax.broadcasted_iota(jnp.int32, (points, points), axis)
        odd = jnp.where(at >= half, 1, 0)
        wave = 2 * jnp.where(at - half * odd >= quarter, at - half * odd - quarter, at - half * odd)
        return at, jnp.where(at == quarter, half, wave + odd).astype(F32) * (2.0 * np.pi / points)

    row, row_wave = grid_index(0)
    column, column_wave = grid_index(1)
    square[...] = jnp.square(row_wave) + jnp.square(column_wave)

    table_cos = even_polynomial(np.cos, np.pi**2, 8)
    table_sinc = even_polynomial(sinc, np.pi**2, 8)

    def frequency(axis, part):
        at = lax.broadcasted_iota(jnp.int32, (half, half), axis)
        if part == 1:
            return jnp.where(at < quarter, 2 * at + 1, points - 1 - 2 * (at - quarter))
        mirrored = jnp.where(at == quarter, half, points - 2 * (at - quarter))
        return jnp.where(at < quarter, 2 * at, mirrored)

    for part in range(2):
        for turned in range(2):
            place = lax.broadcasted_iota(jnp.int32, (half, half), turned)
            product = place * frequency(1 - turned, part)
            wrapped = ((product + half) & (points - 1)) - half
            x = wrapped.astype(F32) * (2.0 * np.pi / points)
            cosine = horner(table_cos, x * x).astype(BF16)
            sine = x * horner(table_sinc, x * x)
            upper, lower = ((-sine).astype(BF16), sine.astype(BF16))
            if turned:
                upper, lower = lower, upper
            tab[turned, part, :half, :half] = cosine
            tab[turned, part, half:, half:] = cosine
            tab[turned, part, :half, half:] = upper
            tab[turned, part, half:, :half] = lower

    def taper(at):
        distance_in = (jnp.minimum(at, points - 1 - at) + 1).astype(F32)
        return jnp.minimum(distance_in * (16.0 / points), 1.0)

    window[...] = taper(row) * taper(column) * (1.0 / points**2)

    pl.semaphore_wait(barrier, shots + 1)
    for front in range(2):
        @pl.when(jnp.logical_and(provider, f == front))
        def _(field=(receiver, source)[front]):
            om[...] = jnp.full((8, points), omegas[fronts - 1], F32)
            send_turn().start()
            send_front(field).start()

    for j in range(levels):
        load_slow(j).wait()
        mean = jnp.mean(slow[j])
        ds[d * levels + j] = (slow[j] - mean).astype(BF16)
        s0[d * levels + j] = jnp.full((8, points), mean, F32)
        send_mean(d * levels + j).start()
        send_slow(d * levels + j).start()

    def fold_into(slot, re, im):
        lo, hi = slice(0, half), slice(half, points)
        for at in range(0, points, CHUNK):
            rows, into = slice(at, at + CHUNK), slice(slot * points + at, slot * points + at + CHUNK)
            for lanes, x in ((lo, re), (hi, im)):
                a, b = x[rows, lo], x[rows, hi]
                st[0, into, lanes] = (a + b).astype(BF16)
                st[1, into, lanes] = (a - b).astype(BF16)

    for index, field in enumerate((source, receiver)):
        load(index, d, field).wait()
        fold_into(index, fbuf.at[index, 0], fbuf.at[index, 1])

    @pl.when(provider)
    def _():
        load(2, fronts - 1, source).wait()

    @pl.when(jnp.logical_not(provider))
    def _():
        send_turn().wait_recv()
        send_field().wait_recv()

    fold_into(2, fbuf.at[2, 0], fbuf.at[2, 1])

    turn_own = omegas[d]
    sign = (2 * f - 1).astype(F32)
    limit = 1.01 * (FASTEST_TURN * SLOWEST) ** 2
    kz_cos = even_polynomial(np.cos, limit, 5)
    kz_sinc = even_polynomial(sinc, limit, 5)
    limit = 1.01 * (FASTEST_TURN * SLOWNESS_SPAN) ** 2
    turn_cos = even_polynomial(np.cos, limit, 4)
    turn_sinc = even_polynomial(sinc, limit, 3)

    def propagator(index, radius_sq, flip):
        def rows(at, count, targets):
            vertical = radius_sq - square[at : at + count, :]
            size = jnp.abs(vertical)
            root = size * lax.rsqrt(jnp.maximum(size, 1e-30))
            positive = vertical >= 0.0
            x = jnp.maximum(vertical, 0.0)
            re = jnp.where(positive, horner(kz_cos, x), jnp.exp2(root * -LOG2_E))
            im = jnp.where(positive, root * horner(kz_sinc, x), 0.0)
            im = im if flip is None else im * flip
            for target in targets:
                pr[index, target : target + count, :] = re
                pi[index, target : target + count, :] = im

        step = quarter // 2
        for at in range(0, quarter, step):
            rows(at, step, (at, at + quarter))
            rows(half + at, step, (half + at, half + quarter + at))
        rows(quarter, 8, (quarter,))

    def correction(index, turn, slow):
        step = quarter // 2
        for at in range(0, points, step):
            x = turn * slow[at : at + step, :].astype(F32)
            y = x * x
            w = window[at : at + step, :]
            cr[index, at : at + step, :] = horner(turn_cos, y) * w
            ci[index, at : at + step, :] = horner(turn_sinc, y) * (x * w)

    def dot(a, b):
        return jnp.dot(a, b, preferred_element_type=F32)

    def transform_all():
        for part in range(2):
            res[part] = dot(st[part], tab[0, part])
        for i in range(3):
            for part in range(2):
                lanes = slice(part * half, (part + 1) * half)
                for at in range(0, half, CHUNK):
                    row = i * points + at
                    top = res[part, row : row + CHUNK, :]
                    bottom = res[part, half + row : half + row + CHUNK, :]
                    for fold, w in ((0, top + bottom), (1, top - bottom)):
                        bb[i, fold, at : at + CHUNK, lanes] = w[:, :half].astype(BF16)
                        bb[i, fold, half + at : half + at + CHUNK, lanes] = w[:, half:].astype(BF16)

    def advance(i, which, sigma):
        for part in range(2):
            base = i * points
            res[part, base : base + points, :] = dot(tab[1, part], bb[i, part])
            for at in range(0, half, CHUNK):
                rows = slice(part * half + at, part * half + at + CHUNK)
                top, bottom = slice(at, at + CHUNK), slice(half + at, half + at + CHUNK)
                re = res[part, base + at : base + at + CHUNK, :]
                im = res[part, base + half + at : base + half + at + CHUNK, :]
                p, q = pr[which, rows, :], pi[which, rows, :]
                if sigma > 0:
                    ww[i, part, top, :] = (re * p - im * q).astype(BF16)
                    ww[i, part, bottom, :] = (re * q + im * p).astype(BF16)
                else:
                    ww[i, part, top, :] = (re * p + im * q).astype(BF16)
                    ww[i, part, bottom, :] = (im * p - re * q).astype(BF16)

    def back(i):
        for part in range(2):
            res[part, i * points : (i + 1) * points, :] = dot(tab[0, part], ww[i, part])
        for at in range(0, points, CHUNK):
            rows = slice(i * points + at, i * points + at + CHUNK)
            even, odd = res[0, rows, :], res[1, rows, :]
            target = at % half
            lanes = slice(0, half) if at < half else slice(half, points)
            for start_row, y in ((0, even + odd), (half, even - odd)):
                into = slice(start_row + target, start_row + target + CHUNK)
                xx[i, 0, into, lanes] = y[:, :half].astype(BF16)
                xx[i, 1, into, lanes] = y[:, half:].astype(BF16)

    def finish(i, which, sigma, emit):
        for part in range(2):
            res[part, i * points : (i + 1) * points, :] = dot(xx[i, part], tab[1, part])
        for at in range(0, points, CHUNK):
            rows = slice(at, at + CHUNK)
            into = slice(i * points + at, i * points + at + CHUNK)
            even, odd = res[0, into, :], res[1, into, :]
            out = []
            for lanes, y in ((slice(0, half), even + odd), (slice(half, points), even - odd)):
                re, im = y[:, :half], y[:, half:]
                c, t = cr[which, rows, lanes], ci[which, rows, lanes]
                if sigma > 0:
                    out.append((re * c - im * t, re * t + im * c))
                else:
                    out.append((re * c + im * t, im * c - re * t))
            for part in range(2):
                a, b = out[0][part], out[1][part]
                lanes = slice(part * half, (part + 1) * half)
                st[0, into, lanes] = (a + b).astype(BF16)
                st[1, into, lanes] = (a - b).astype(BF16)
            emit(rows, out)

    def combine(z):
        send_image(z).wait_recv()
        send_shared(z).wait_recv()
        total = acc[lax.rem(z, 2), f] + accr[z].astype(F32)
        total += shq[z, f, 0].astype(F32) * shr[z, 0].astype(F32)
        total += shq[z, f, 1].astype(F32) * shr[z, 1].astype(F32)
        mine = lax.div(z, levels) == d

        @pl.when(mine)
        def _():
            chip[lax.rem(z, levels)] = total

        @pl.when(jnp.logical_not(mine))
        def _():
            xsend[lax.rem(z, levels)] = total.astype(BF16)
            send_section(z).start()

    def place(z):
        j = lax.rem(z, levels)
        send_section(z).wait_recv()
        total = (chip[j] + xrecv[j].astype(F32)).astype(BF16)
        columns = lax.broadcasted_iota(jnp.int32, (TILE, points), 0)
        places = lax.broadcasted_iota(jnp.int32, (TILE, points), 1)
        for step in [*range(1, shots), 0]:
            owner = lax.rem(s + step, shots)
            chosen = places == columns + (owner * TILE - start[0])
            chosen = jnp.where(chosen, 1.0, 0.0).astype(BF16)
            zsend[j, owner] = dot(chosen, total).astype(BF16)
            if step > 0:
                send_columns(j, step).start()

    def one_level(z, carry):
        mine = lax.div(z, levels) == d

        @pl.when(jnp.logical_not(mine))
        def _():
            send_mean(z).wait_recv()

        mean = s0[z][0:1, :]
        turn_shared = om[0:1, :]
        transform_all()
        propagator(1, jnp.square(turn_shared * mean), sign)
        propagator(0, jnp.square(turn_own * mean), None)
        advance(2, 1, 1)
        back(2)
        advance(0, 0, -1)
        advance(1, 0, 1)

        @pl.when(jnp.logical_not(mine))
        def _():
            send_slow(z).wait_recv()

        @pl.when(z >= 1)
        def _():
            combine(z - 1)

        def emit_shared(rows, out):
            for side in range(2):
                for part in range(2):
                    shq[z, side, part, rows, :] = out[side][part].astype(BF16)

        def emit_first(rows, out):
            for side in range(2):
                for part in range(2):
                    uq[side, part, rows, :] = out[side][part]

        def emit_second(rows, out):
            for side in range(2):
                product = uq[side, 0, rows, :] * out[side][0] + uq[side, 1, rows, :] * out[side][1]
                acc[lax.rem(z, 2), side, rows, :] = product
                accb[z, side, rows, :] = product.astype(BF16)

        correction(1, sign * turn_shared, ds.at[z])
        finish(2, 1, 1, emit_shared)
        send_shared(z).start()
        correction(0, turn_own, ds.at[z])
        back(0)
        back(1)
        finish(0, 0, -1, emit_first)
        finish(1, 0, 1, emit_second)
        send_image(z).start()

        before = z - 2 + d

        @pl.when(jnp.logical_and(before >= d * levels, before < (d + 1) * levels))
        def _():
            place(before)

        return carry

    lax.fori_loop(0, total_levels, one_level, 0)
    last = total_levels - 1
    combine(last)

    @pl.when(lax.div(last, levels) == d)
    def _():
        place(last)

    for j in range(levels):
        total = zsend[j, s].astype(F32)
        for step in range(1, shots):
            recv_columns(j, step).wait_recv()
            total += zrecv[j, lax.rem(s + step, shots)].astype(F32)
        image[pl.ds(j, TILE, stride=levels), :] = total

    @pl.when(provider)
    def _():
        send_turn().wait_send()
        send_field().wait_send()

    for j in range(levels):
        send_mean(d * levels + j).wait_send()
        send_slow(d * levels + j).wait_send()
        send_section((1 - d) * levels + j).wait_send()
        for step in range(1, shots):
            send_columns(j, step).wait_send()
    for z in range(total_levels):
        send_image(z).wait_send()
        send_shared(z).wait_send()


def migrate(source, receiver, slowness, omegas, shot_start):
    points = source.shape[-1]
    fronts = source.shape[1]
    levels = slowness.shape[1]
    shots = lax.axis_size("shot")
    total = 2 * levels
    half = points // 2
    full = (points, points)
    side = (points, half)
    vmem, sem = pltpu.VMEM, pltpu.SemaphoreType.DMA
    in_vmem = pl.BlockSpec(memory_space=pltpu.VMEM)
    in_smem = pl.BlockSpec(memory_space=pltpu.SMEM)
    anywhere = pl.BlockSpec(memory_space=pltpu.HBM)
    return pl.pallas_call(
        functools.partial(migrate_kernel, (points, levels, shots, fronts)),
        out_shape=jax.ShapeDtypeStruct((TILE * levels, half), F32),
        in_specs=[anywhere, anywhere, anywhere, in_smem, in_smem],
        out_specs=in_vmem,
        scratch_shapes=[
            vmem((2, 2) + full, BF16),
            vmem((levels,) + full, F32),
            vmem(full, F32),
            vmem(full, F32),
            vmem((2, 3 * points, points), F32),
            vmem((3, 2) + full, F32),
            vmem((2, 3 * points, points), BF16),
            vmem((total,) + full, BF16),
            vmem((total, 8, points), F32),
            vmem((8, points), F32),
            vmem((2,) + full, F32),
            vmem((2,) + full, F32),
            vmem((2,) + full, F32),
            vmem((2,) + full, F32),
            vmem((3, 2) + full, BF16),
            vmem((3, 2) + full, BF16),
            vmem((3, 2) + full, BF16),
            vmem((2, 2) + side, F32),
            vmem((2, 2) + side, F32),
            vmem((total, 2) + side, BF16),
            vmem((total, 2, 2) + side, BF16),
            vmem((total,) + side, BF16),
            vmem((total, 2) + side, BF16),
            vmem((levels,) + side, F32),
            vmem((levels,) + side, BF16),
            vmem((levels,) + side, BF16),
            vmem((levels, shots, TILE, half), BF16),
            vmem((levels, shots, TILE, half), BF16),
            sem((3,)),
            sem((levels,)),
            sem((2, total)),
            sem((2, total)),
            sem((2, 1)),
            sem((2, 1)),
            sem((2, total)),
            sem((2, total)),
            sem((2, levels)),
            sem((levels, shots)),
            sem((levels, shots)),
        ],
        compiler_params=pltpu.CompilerParams(
            collective_id=0, has_side_effects=True, vmem_limit_bytes=55000 * 1024
        ),
        name="migrate",
    )(source, receiver, slowness, omegas.reshape(-1), shot_start).reshape(TILE, levels, half)


def solution(mesh):
    sizes = mesh.shape

    def per_device(source, receiver, slowness, *rest):
        if sizes["depth"] == 2 and sizes["freq"] == 2 and source.shape[1] == 3 and slowness.shape[1] > 1:
            return migrate(source, receiver, slowness, *rest)
        return local(source, receiver, slowness, *rest)

    return jax.shard_map(
        per_device,
        mesh=mesh,
        in_specs=(
            P(("groups", "shot"), "freq", None, None, None),
            P(("groups", "shot"), "freq", None, None, None),
            P(("groups", "shot"), "depth", None, None),
            P(("groups", "shot"), "freq"),
            P(("groups", "shot")),
        ),
        out_specs=P(("groups", "shot"), "depth", "freq"),
        check_vma=False,
    )
```
